32 devices in a mesh: cin: 4 (over z), cout: 2 (over y), sp: 4 (over x, core).
Axes of the slice: x: 2, y: 2, z: 4, core: 2. Of those that a mesh axis runs over, the one named last changes fastest.
Arguments:
- activations: bfloat16 [512, 4, 32, 128], P('cin', 'sp', 'cout'), may hold values from -6 to 6
- weights: bfloat16 [3, 3, 3, 512, 512], P(None, None, None, 'cin', 'cout'), may hold values from -0.0546875 to 0.0546875
- out_grad: bfloat16 [512, 4, 32, 128], P('cout', 'sp', 'cin'), may hold values from -6 to 6
Outputs:
- output: bfloat16 [512, 4, 32, 128], P('cout', 'sp', 'cin')
- in_grad: bfloat16 [512, 4, 32, 128], P('cin', 'sp', 'cout')
- weight_grad: bfloat16 [3, 3, 3, 512, 512], P(None, None, None, 'cin', 'cout')
The draws below stay inside these ranges and needn't reach their ends.
All inputs are finite; a program needn't handle non-finite values.
Results may differ from the reference program's by a relative error of at most 0.001.
Values may be sent and summed in bfloat16 or wider, within the bound.
A program may use at most 64 MiB of HBM per device.

```python
import math
import jax
import jax.numpy as jnp
from jax import lax

CIN = 512
COUT = 512
H = 32
W = 128
DEPTH = 4
VOXELS = 16384


def spiked(values, rng, source, target, parts, factor):
    def block_of(axis_at):
        return (jnp.arange(values.shape[axis_at]) // (values.shape[axis_at] // parts)).reshape((-1,) + (1,) * (values.ndim - 1 - axis_at))

    first = jax.random.permutation(rng, parts)[block_of(target)]
    far = (block_of(target) + parts // 2) % parts
    return jnp.where((block_of(source) == first) | (block_of(source) == far), factor * values, values)


def block_scale(rng, extent, pieces, low, high):
    loudness, own = 1.0, jax.random.fold_in(rng, 6)
    for position, parts in pieces:
        steps = jnp.exp(jax.random.uniform(jax.random.fold_in(own, position), (parts,), jnp.float32, low / len(pieces), high / len(pieces)))
        loudness = loudness * jnp.repeat(steps, extent[position] // parts).reshape([-1 if axis == position else 1 for axis in range(len(extent))])
    return loudness


def normal_values(stream_key, extent, deviation, limit, cuts=(), held_as=jnp.bfloat16):
    values = jax.random.normal(stream_key, extent, jnp.float32) * deviation
    if len(cuts) > 0:
        values = block_scale(stream_key, extent, cuts, -0.22, 0.18) * values
    return jnp.clip(values, min=-limit, max=limit).astype(held_as)


def heavy_noise(own_key, shape, scale, reach, pieces, heavy, kind=jnp.bfloat16):
    array = scale * jax.random.normal(own_key, shape, jnp.float32)
    if pieces:
        array = array * block_scale(own_key, shape, pieces, -0.22, 0.18)
    return jnp.clip(spiked(array, jax.random.fold_in(own_key, 3), *heavy), -reach, reach).astype(kind)


def setup_inputs(seed: int = 0) -> dict:
    keys = jax.random.split(jax.random.key(seed), 4)
    activations = heavy_noise(keys[0], (CIN, DEPTH, H, W), 1.0, 6.0, ((0, 4), (1, 4), (2, 2)), (0, 2, 4, 2.0))
    weights = normal_values(keys[1], (3, 3, 3, CIN, COUT), (27 * CIN) ** -0.5, 0.0546875, ((3, 4), (4, 2)))
    out_grad = heavy_noise(keys[2], (COUT, DEPTH, H, W), 1.0, 6.0, ((0, 2), (1, 4), (2, 4)), (0, 2, 4, 2.0))
    return {"activations": activations, "weights": weights, "out_grad": out_grad}


def conv_same(field, kernel):
    return lax.conv_general_dilated(field[None], kernel, (1, 1, 1), [(1, 1), (1, 1), (1, 1)], dimension_numbers=('NCDHW', 'DHWIO', 'NCDHW'), precision=lax.Precision.HIGHEST)[0]

def reference(activations, weights, out_grad):
    x_float = activations.astype(jnp.float32)
    w_float = weights.astype(jnp.float32)
    g_float = out_grad.astype(jnp.float32)
    output = conv_same(x_float, w_float).astype(jnp.bfloat16)
    flipped = jnp.transpose(w_float[::-1, ::-1, ::-1], (0, 1, 2, 4, 3))
    in_grad = conv_same(g_float, flipped).astype(jnp.bfloat16)
    padded = jnp.pad(x_float, ((0, 0), (1, 1), (1, 1), (1, 1)))
    tap_terms = []
    for a in range(3):
        for b in range(3):
            for c in range(3):
                window = padded[:, a:a + DEPTH, b:b + H, c:c + W]
                tap_terms.append(jnp.einsum('cdhw,odhw->co', window, g_float, precision=lax.Precision.HIGHEST))
    summed = jnp.stack(tap_terms).reshape(3, 3, 3, CIN, COUT)
    weight_grad = (summed * (1.0 / math.sqrt(VOXELS))).astype(jnp.bfloat16)
    return (output, in_grad, weight_grad)
```

```python
import functools
import math

import jax
import jax.numpy as jnp
from jax import lax
from jax.experimental import pallas as pl
from jax.experimental.pallas import tpu as pltpu
from jax.sharding import PartitionSpec as P

F32 = jnp.float32
BF16 = jnp.bfloat16
VMEM_BYTES = 56 * 1024 * 1024


def right_pairs(first, last):
    return [(i, i + 1) for i in range(first, last)]


def left_pairs(first, last):
    return [(i + 1, i) for i in range(first, last)]


def line_gather(block, axis):
    count = lax.axis_size(axis)
    from_low, from_high = [], []
    moving_up, moving_down = block, block
    for step in range(1, count):
        moving_up = lax.ppermute(moving_up, axis, right_pairs(step - 1, count - 1))
        moving_down = lax.ppermute(moving_down, axis, left_pairs(0, count - step))
        from_low.insert(0, moving_up)
        from_high.append(moving_down)
    if count == 2:
        low, high = from_low[0], from_high[0]
        first = lax.axis_index(axis) == 0
        return jnp.concatenate(
            [jnp.where(first, block, low), jnp.where(first, high, block)], axis=0
        )
    around = jnp.concatenate(from_low + [block] + from_high, axis=0)
    extent = block.shape[0]
    start = (count - 1 - lax.axis_index(axis)) * extent
    return lax.dynamic_slice_in_dim(around, start, count * extent, axis=0)


def line_reduce_scatter(partial, axis):
    count = lax.axis_size(axis)
    me = lax.axis_index(axis)
    extent = partial.shape[0] // count

    def chunk(index):
        index = jnp.clip(index, 0, count - 1)
        return lax.dynamic_slice_in_dim(partial, index * extent, extent, axis=0)

    up, down = None, None
    for step in range(count - 1):
        send_up = chunk(count - 1 - step + me)
        send_down = chunk(step - (count - 1) + me)
        if up is not None:
            send_up = send_up + up
            send_down = send_down + down
        up = lax.ppermute(send_up, axis, right_pairs(0, step + 1))
        down = lax.ppermute(send_down, axis, left_pairs(count - 2 - step, count - 1))
    return chunk(me) + up + down


def exchange(value, axis, distance):
    count = lax.axis_size(axis)
    return lax.ppermute(value, axis, [(i, i ^ distance) for i in range(count)])


def reduce_all(partial, axis, scale):
    count = lax.axis_size(axis)
    me = lax.axis_index(axis)
    held = partial
    distance = 1
    while distance < count:
        half = held.shape[1] // 2
        bit = (me // distance) % 2
        mine = lax.dynamic_slice_in_dim(held, bit * half, half, axis=1)
        other = lax.dynamic_slice_in_dim(held, (1 - bit) * half, half, axis=1)
        held = mine + exchange(other, axis, distance)
        distance *= 2
    held = (held * scale).astype(BF16)
    while distance > 1:
        distance //= 2
        bit = (me // distance) % 2
        other = exchange(held, axis, distance)
        low = jnp.where(bit == 0, held, other)
        high = jnp.where(bit == 0, other, held)
        held = jnp.concatenate([low, high], axis=1)
    return held


def shifted(row, offset):
    if offset == 0:
        return row
    width = row.shape[1]
    wide = pltpu.roll(row.astype(F32), (-offset) % width, 1)
    lane = lax.broadcasted_iota(jnp.int32, wide.shape, 1)
    edge = width - 1 if offset > 0 else 0
    return jnp.where(lane == edge, 0.0, wide).astype(row.dtype)


def stack_shifts(planes, stacked):
    rows, channels, width = planes[0].shape
    for a, plane in enumerate(planes):
        stacked[a, 0] = jnp.zeros((3 * channels, width), BF16)
        stacked[a, rows + 1] = jnp.zeros((3 * channels, width), BF16)

        def one(r, carry, a=a, plane=plane):
            row = plane[r]
            for c in range(3):
                stacked[a, r + 1, pl.ds(c * channels, channels)] = shifted(row, c - 1)
            return carry

        lax.fori_loop(0, rows, one, 0)


def output_kernel(low, mid, high, kernel, out, stacked):
    stack_shifts((low, mid, high), stacked)
    taps = [(a, b) for a in range(3) for b in range(3)]

    def pair(step, carry):
        r = step * 2
        total = None
        for group in (taps[0:4], taps[4:8], taps[8:9]):
            left = jnp.concatenate([kernel[a * 3 + b] for a, b in group], axis=1)
            right = jnp.concatenate(
                [
                    jnp.concatenate([stacked[a, r + b], stacked[a, r + b + 1]], axis=1)
                    for a, b in group
                ],
                axis=0,
            )
            term = jnp.dot(left, right, preferred_element_type=F32)
            total = term if total is None else total + term
        width = mid.shape[2]
        out[r] = total[:, :width]
        out[r + 1] = total[:, width:]
        return carry

    lax.fori_loop(0, mid.shape[0] // 2, pair, 0)


def input_grad_kernel(low, mid, high, kernel, out, padded):
    rows, channels, width = mid.shape
    for a, plane in enumerate((low, mid, high)):
        padded[a, 0] = jnp.zeros((channels, width), BF16)
        padded[a, rows + 1] = jnp.zeros((channels, width), BF16)

        def one(r, carry, a=a, plane=plane):
            padded[a, r + 1] = plane[r]
            return carry

        lax.fori_loop(0, rows, one, 0)
    inner = out.shape[1]

    def pair(step, carry):
        r = step * 2
        total = None
        for a in range(3):
            left = jnp.concatenate([kernel[a * 3 + b] for b in range(3)], axis=1)
            right = jnp.concatenate(
                [
                    jnp.concatenate([padded[2 - a, r + 2 - b], padded[2 - a, r + 3 - b]], axis=1)
                    for b in range(3)
                ],
                axis=0,
            )
            term = jnp.dot(left, right, preferred_element_type=F32)
            total = term if total is None else total + term
        for k in range(2):
            part = total[:, k * width : (k + 1) * width]
            lane = lax.broadcasted_iota(jnp.int32, (inner, width), 1)
            ahead = pltpu.roll(part[0:inner], width - 1, 1)
            behind = pltpu.roll(part[2 * inner : 3 * inner], 1, 1)
            out[r + k] = (
                part[inner : 2 * inner]
                + jnp.where(lane == width - 1, 0.0, ahead)
                + jnp.where(lane == 0, 0.0, behind)
            )
        return carry

    lax.fori_loop(0, rows // 2, pair, 0)


def weight_grad_kernel(low, mid, high, grad, out, stacked, turned):
    rows = mid.shape[0]
    stack_shifts((low, mid, high), stacked)

    def turn(r, carry):
        turned[r] = grad[r].T
        return carry

    lax.fori_loop(0, rows, turn, 0)
    span = 8

    for a in range(3):

        def tap(b, carry, a=a):
            def part(k):
                left = jnp.concatenate(
                    [stacked[a, b + k * span + j] for j in range(span)], axis=1
                )
                right = jnp.concatenate([turned[k * span + j] for j in range(span)], axis=0)
                return jnp.dot(left, right, preferred_element_type=F32)

            total = part(0)
            for k in range(1, rows // span):
                total = total + part(k)
            out[a * 3 + b] = total
            return carry

        lax.fori_loop(0, 3, tap, 0)


def call(kernel, operands, out_shape, scratch):
    flops = 2 * 27 * 128 * 256 * 4096
    return pl.pallas_call(
        kernel,
        out_shape=jax.ShapeDtypeStruct(out_shape, F32),
        in_specs=[pl.BlockSpec(memory_space=pltpu.VMEM)] * len(operands),
        out_specs=pl.BlockSpec(memory_space=pltpu.VMEM),
        scratch_shapes=[pltpu.VMEM(shape, BF16) for shape in scratch],
        compiler_params=pltpu.CompilerParams(vmem_limit_bytes=VMEM_BYTES),
        cost_estimate=pl.CostEstimate(flops=flops, bytes_accessed=8 << 20, transcendentals=0),
    )(*operands)


def plain_conv(planes, kernel):
    return lax.conv_general_dilated(
        planes.transpose(2, 0, 1, 3)[None],
        kernel,
        (1, 1, 1),
        [(0, 0), (1, 1), (1, 1)],
        dimension_numbers=("NCDHW", "DHWIO", "NCDHW"),
        preferred_element_type=F32,
    )[0, :, 0].transpose(1, 0, 2)


def local_output(planes, weights):
    ci, co = weights.shape[3:]
    rows, _, width = planes[1].shape
    if ci % 128 or co % 128:
        return plain_conv(jnp.stack(planes), weights)
    kernel = weights.reshape(9, 3 * ci, co).transpose(0, 2, 1)
    return call(
        output_kernel, (*planes, kernel), (rows, co, width), [(3, rows + 2, 3 * ci, width)]
    )


def local_input_grad(planes, weights):
    ci, co = weights.shape[3:]
    rows, _, width = planes[1].shape
    if ci % 128 or co % 128:
        flipped = jnp.transpose(weights[::-1, ::-1, ::-1], (0, 1, 2, 4, 3))
        return plain_conv(jnp.stack(planes), flipped)
    kernel = weights.reshape(9, 3 * ci, co)
    return call(
        input_grad_kernel, (*planes, kernel), (rows, ci, width), [(3, rows + 2, co, width)]
    )


def local_weight_grad(planes, grad):
    rows, ci, width = planes[1].shape
    co = grad.shape[1]
    if ci % 128 or co % 128:
        padded = jnp.pad(jnp.stack(planes), ((0, 0), (1, 1), (0, 0), (1, 1)))
        terms = [
            jnp.einsum(
                "rcw,row->co",
                padded[a, b : b + rows, :, c : c + width],
                grad,
                preferred_element_type=F32,
            )
            for a in range(3)
            for b in range(3)
            for c in range(3)
        ]
        return jnp.stack(terms)
    out = call(
        weight_grad_kernel,
        (*planes, grad),
        (9, 3 * ci, co),
        [(3, rows + 2, 3 * ci, width), (rows, width, co)],
    )
    return out.reshape(27, ci, co)


def with_neighbours(plane):
    count = lax.axis_size("sp")
    low = lax.ppermute(plane, "sp", right_pairs(0, count - 1))
    high = lax.ppermute(plane, "sp", left_pairs(0, count - 1))
    return low, plane, high


def body(activations, weights, out_grad):
    grad_rows = out_grad[:, 0].transpose(1, 0, 2)
    x_rows = activations[:, 0].transpose(1, 0, 2)
    x_panel = line_gather(x_rows, "cout")
    g_panel = line_gather(grad_rows, "cin")
    x_planes = with_neighbours(x_panel)
    g_planes = with_neighbours(g_panel)
    partial_out = local_output(x_planes, weights)
    output = line_reduce_scatter(partial_out, "cin")
    output = output.transpose(1, 0, 2).astype(BF16)[:, None]
    partial_weights = local_weight_grad(x_planes, g_panel)
    voxels = lax.axis_size("sp") * g_panel.shape[0] * g_panel.shape[2]
    weight_grad = reduce_all(partial_weights, "sp", 1.0 / math.sqrt(voxels))
    partial_in = local_input_grad(g_planes, weights)
    in_grad = line_reduce_scatter(partial_in, "cout")
    in_grad = in_grad.transpose(1, 0, 2).astype(BF16)[:, None]
    return (output, in_grad, weight_grad.reshape(weights.shape))


def solution(mesh):
    return jax.shard_map(
        body,
        mesh=mesh,
        in_specs=(
            P("cin", "sp", "cout", None),
            P(None, None, None, "cin", "cout"),
            P("cout", "sp", "cin", None),
        ),
        out_specs=(
            P("cout", "sp", "cin", None),
            P("cin", "sp", "cout", None),
            P(None, None, None, "cin", "cout"),
        ),
        check_vma=False,
    )
```

```python
import functools
import math

import jax
import jax.numpy as jnp
from jax import lax
from jax.experimental import pallas as pl
from jax.experimental.pallas import tpu as pltpu
from jax.sharding import PartitionSpec as P

F32 = jnp.float32
BF16 = jnp.bfloat16
VMEM_BYTES = 56 * 1024 * 1024


def right_pairs(first, last):
    return [(i, i + 1) for i in range(first, last)]


def left_pairs(first, last):
    return [(i + 1, i) for i in range(first, last)]


def line_gather(block, axis):
    count = lax.axis_size(axis)
    from_low, from_high = [], []
    moving_up, moving_down = block, block
    for step in range(1, count):
        moving_up = lax.ppermute(moving_up, axis, right_pairs(step - 1, count - 1))
        moving_down = lax.ppermute(moving_down, axis, left_pairs(0, count - step))
        from_low.insert(0, moving_up)
        from_high.append(moving_down)
    if count == 2:
        low, high = from_low[0], from_high[0]
        first = lax.axis_index(axis) == 0
        return jnp.concatenate(
            [jnp.where(first, block, low), jnp.where(first, high, block)], axis=0
        )
    around = jnp.concatenate(from_low + [block] + from_high, axis=0)
    extent = block.shape[0]
    start = (count - 1 - lax.axis_index(axis)) * extent
    return lax.dynamic_slice_in_dim(around, start, count * extent, axis=0)


def line_reduce_scatter(partial, axis):
    count = lax.axis_size(axis)
    me = lax.axis_index(axis)
    extent = partial.shape[0] // count

    def chunk(index):
        index = jnp.clip(index, 0, count - 1)
        return lax.dynamic_slice_in_dim(partial, index * extent, extent, axis=0)

    up, down = None, None
    for step in range(count - 1):
        send_up = chunk(count - 1 - step + me)
        send_down = chunk(step - (count - 1) + me)
        if up is not None:
            send_up = send_up + up
            send_down = send_down + down
        up = lax.ppermute(send_up, axis, right_pairs(0, step + 1))
        down = lax.ppermute(send_down, axis, left_pairs(count - 2 - step, count - 1))
    return chunk(me) + up + down


def exchange(value, axis, distance):
    count = lax.axis_size(axis)
    return lax.ppermute(value, axis, [(i, i ^ distance) for i in range(count)])


def reduce_all(partial, axis, scale):
    count = lax.axis_size(axis)
    me = lax.axis_index(axis)
    held = partial
    distance = 1
    while distance < count:
        half = held.shape[1] // 2
        bit = (me // distance) % 2
        mine = lax.dynamic_slice_in_dim(held, bit * half, half, axis=1)
        other = lax.dynamic_slice_in_dim(held, (1 - bit) * half, half, axis=1)
        held = mine + exchange(other, axis, distance)
        distance *= 2
    held = (held * scale).astype(BF16)
    while distance > 1:
        distance //= 2
        bit = (me // distance) % 2
        other = exchange(held, axis, distance)
        low = jnp.where(bit == 0, held, other)
        high = jnp.where(bit == 0, other, held)
        held = jnp.concatenate([low, high], axis=1)
    return held


def shifted(row, offset):
    if offset == 0:
        return row
    width = row.shape[1]
    wide = pltpu.roll(row.astype(F32), (-offset) % width, 1)
    lane = lax.broadcasted_iota(jnp.int32, wide.shape, 1)
    edge = width - 1 if offset > 0 else 0
    return jnp.where(lane == edge, 0.0, wide).astype(row.dtype)


def stack_shifts(planes, stacked):
    rows, channels, width = planes[0].shape
    for a, plane in enumerate(planes):
        stacked[a, 0] = jnp.zeros((3 * channels, width), BF16)
        stacked[a, rows + 1] = jnp.zeros((3 * channels, width), BF16)

        def one(r, carry, a=a, plane=plane):
            row = plane[r]
            for c in range(3):
                stacked[a, r + 1, pl.ds(c * channels, channels)] = shifted(row, c - 1)
            return carry

        lax.fori_loop(0, rows, one, 0)


def output_kernel(low, mid, high, kernel, out, stacked):
    stack_shifts((low, mid, high), stacked)
    taps = [(a, b) for a in range(3) for b in range(3)]

    def pair(step, carry):
        r = step * 2
        total = None
        for group in (taps[0:4], taps[4:8], taps[8:9]):
            left = jnp.concatenate([kernel[a * 3 + b] for a, b in group], axis=1)
            right = jnp.concatenate(
                [
                    jnp.concatenate([stacked[a, r + b], stacked[a, r + b + 1]], axis=1)
                    for a, b in group
                ],
                axis=0,
            )
            term = jnp.dot(left, right, preferred_element_type=F32)
            total = term if total is None else total + term
        width = mid.shape[2]
        out[r] = total[:, :width]
        out[r + 1] = total[:, width:]
        return carry

    lax.fori_loop(0, mid.shape[0] // 2, pair, 0)


def input_grad_kernel(low, mid, high, kernel, out, padded):
    rows, channels, width = mid.shape
    for a, plane in enumerate((low, mid, high)):
        padded[a, 0] = jnp.zeros((channels, width), BF16)
        padded[a, rows + 1] = jnp.zeros((channels, width), BF16)

        def one(r, carry, a=a, plane=plane):
            padded[a, r + 1] = plane[r]
            return carry

        lax.fori_loop(0, rows, one, 0)
    inner = out.shape[1]

    def pair(step, carry):
        r = step * 2
        total = None
        for a in range(3):
            left = jnp.concatenate([kernel[a * 3 + b] for b in range(3)], axis=1)
            right = jnp.concatenate(
                [
                    jnp.concatenate([padded[2 - a, r + 2 - b], padded[2 - a, r + 3 - b]], axis=1)
                    for b in range(3)
                ],
                axis=0,
            )
            term = jnp.dot(left, right, preferred_element_type=F32)
            total = term if total is None else total + term
        for k in range(2):
            part = total[:, k * width : (k + 1) * width]
            lane = lax.broadcasted_iota(jnp.int32, (inner, width), 1)
            ahead = pltpu.roll(part[0:inner], width - 1, 1)
            behind = pltpu.roll(part[2 * inner : 3 * inner], 1, 1)
            out[r + k] = (
                part[inner : 2 * inner]
                + jnp.where(lane == width - 1, 0.0, ahead)
                + jnp.where(lane == 0, 0.0, behind)
            )
        return carry

    lax.fori_loop(0, rows // 2, pair, 0)


def weight_grad_kernel(low, mid, high, grad, out, stacked, turned):
    rows = mid.shape[0]
    stack_shifts((low, mid, high), stacked)

    def turn(r, carry):
        turned[r] = grad[r].T
        return carry

    lax.fori_loop(0, rows, turn, 0)
    span = 8

    for a in range(3):

        def tap(b, carry, a=a):
            def part(k):
                left = jnp.concatenate(
                    [stacked[a, b + k * span + j] for j in range(span)], axis=1
                )
                right = jnp.concatenate([turned[k * span + j] for j in range(span)], axis=0)
                return jnp.dot(left, right, preferred_element_type=F32)

            total = part(0)
            for k in range(1, rows // span):
                total = total + part(k)
            out[a * 3 + b] = total
            return carry

        lax.fori_loop(0, 3, tap, 0)


def call(kernel, operands, out_shape, scratch):
    flops = 2 * 27 * 128 * 256 * 4096
    return pl.pallas_call(
        kernel,
        out_shape=jax.ShapeDtypeStruct(out_shape, F32),
        in_specs=[pl.BlockSpec(memory_space=pltpu.VMEM)] * len(operands),
        out_specs=pl.BlockSpec(memory_space=pltpu.VMEM),
        scratch_shapes=[pltpu.VMEM(shape, BF16) for shape in scratch],
        compiler_params=pltpu.CompilerParams(vmem_limit_bytes=VMEM_BYTES),
        cost_estimate=pl.CostEstimate(flops=flops, bytes_accessed=8 << 20, transcendentals=0),
    )(*operands)


def plain_conv(planes, kernel):
    return lax.conv_general_dilated(
        planes.transpose(2, 0, 1, 3)[None],
        kernel,
        (1, 1, 1),
        [(0, 0), (1, 1), (1, 1)],
        dimension_numbers=("NCDHW", "DHWIO", "NCDHW"),
        preferred_element_type=F32,
    )[0, :, 0].transpose(1, 0, 2)


def local_output(planes, weights):
    ci, co = weights.shape[3:]
    rows, _, width = planes[1].shape
    if ci % 128 or co % 128:
        return plain_conv(jnp.stack(planes), weights)
    kernel = weights.reshape(9, 3 * ci, co).transpose(0, 2, 1)
    return call(
        output_kernel, (*planes, kernel), (rows, co, width), [(3, rows + 2, 3 * ci, width)]
    )


def local_input_grad(planes, weights):
    ci, co = weights.shape[3:]
    rows, _, width = planes[1].shape
    if ci % 128 or co % 128:
        flipped = jnp.transpose(weights[::-1, ::-1, ::-1], (0, 1, 2, 4, 3))
        return plain_conv(jnp.stack(planes), flipped)
    kernel = weights.reshape(9, 3 * ci, co)
    return call(
        input_grad_kernel, (*planes, kernel), (rows, ci, width), [(3, rows + 2, co, width)]
    )


def local_weight_grad(planes, grad):
    rows, ci, width = planes[1].shape
    co = grad.shape[1]
    if ci % 128 or co % 128:
        padded = jnp.pad(jnp.stack(planes), ((0, 0), (1, 1), (0, 0), (1, 1)))
        terms = [
            jnp.einsum(
                "rcw,row->co",
                padded[a, b : b + rows, :, c : c + width],
                grad,
                preferred_element_type=F32,
            )
            for a in range(3)
            for b in range(3)
            for c in range(3)
        ]
        return jnp.stack(terms)
    out = call(
        weight_grad_kernel,
        (*planes, grad),
        (9, 3 * ci, co),
        [(3, rows + 2, 3 * ci, width), (rows, width, co)],
    )
    return out.reshape(27, ci, co)


def with_neighbours(plane):
    count = lax.axis_size("sp")
    low = lax.ppermute(plane, "sp", right_pairs(0, count - 1))
    high = lax.ppermute(plane, "sp", left_pairs(0, count - 1))
    return low, plane, high


def whole_kernel(
    x_own, g_own, kernel_t, kernel, out, dx_out, dw_out,
    xp, stacked, gp, turned, op, o_recv, dwp, dw_half, dw_quarter, dwb, dxp, dx_recv, send, recv,
):
    z, y, s = lax.axis_index("cin"), lax.axis_index("cout"), lax.axis_index("sp")
    nz, ns = 4, 4
    rows, ci, width = xp.shape[1:]
    co = gp.shape[2]
    g_rows, x_rows = rows // nz, rows // 2
    b0, b1 = s % 2, s // 2
    used = [0]
    sent = []

    def link(src, dst, axis, target, when=None):
        slot = used[0]
        used[0] += 1
        copy = pltpu.make_async_remote_copy(
            src_ref=src, dst_ref=dst, send_sem=send.at[slot], recv_sem=recv.at[slot],
            device_id={axis: target}, device_id_type=pl.DeviceIdType.MESH,
        )

        def start():
            if when is None:
                copy.start()
            else:
                pl.when(when)(copy.start)

        sent.append((copy, when))
        return slot, start

    def landed(slot, dst, axis, target, when=None):
        copy = pltpu.make_async_remote_copy(
            src_ref=dst, dst_ref=dst, send_sem=send.at[slot], recv_sem=recv.at[slot],
            device_id={axis: target}, device_id_type=pl.DeviceIdType.MESH,
        )
        if when is None:
            copy.wait_recv()
        else:
            pl.when(when)(copy.wait_recv)

    partners = [
        ("cin", z - 1, z > 0), ("cin", z + 1, z < nz - 1), ("cout", 1 - y, None),
        ("sp", s - 1, s > 0), ("sp", s + 1, s < ns - 1), ("sp", (s + 2) % 4, None),
    ]
    barrier = pltpu.get_barrier_semaphore()

    def each(action):
        for axis, target, when in partners:
            if when is None:
                action(axis, target)
            else:
                pl.when(when)(functools.partial(action, axis, target))

    each(lambda axis, target: pl.semaphore_signal(
        barrier, inc=1, device_id={axis: target}, device_id_type=pl.DeviceIdType.MESH))
    peers = 2
    for inside in (z > 0, z < nz - 1, s > 0, s < ns - 1):
        peers = peers + jnp.where(inside, 1, 0)
    pl.semaphore_wait(barrier, peers)

    x_slot, go = link(x_own, xp.at[1, pl.ds(y * x_rows, x_rows)], "cout", 1 - y)
    go()

    def g_block(index):
        return gp.at[1, pl.ds(1 + index * g_rows, g_rows)]

    up_slots, down_slots = [], []

    def gather_send(t):
        up_source = g_own if t == 1 else g_block(z - (t - 1))
        slot, go = link(up_source, g_block(z - (t - 1)), "cin", z + 1, (z >= t - 1) & (z < nz - 1))
        go()
        up_slots.append(slot)
        down_source = g_own if t == 1 else g_block(z + (t - 1))
        slot, go = link(down_source, g_block(z + (t - 1)), "cin", z - 1, (z <= nz - t) & (z > 0))
        go()
        down_slots.append(slot)

    def gather_wait(t):
        landed(up_slots[t - 1], g_block(z - t), "cin", z - 1, z >= t)
        landed(down_slots[t - 1], g_block(z + t), "cin", z + 1, z <= nz - 1 - t)

    gather_send(1)

    def copy_rows(count, store):
        def one(r, carry):
            store(r)
            return carry

        lax.fori_loop(0, count, one, 0)

    def put_x(r):
        xp[1, y * x_rows + r] = x_own[r]

    def put_g(r):
        gp[1, 1 + z * g_rows + r] = g_own[r]

    copy_rows(x_rows, put_x)
    copy_rows(g_rows, put_g)
    for a in range(3):
        gp[a, 0] = jnp.zeros((co, width), BF16)
        gp[a, rows + 1] = jnp.zeros((co, width), BF16)
        stacked[a, 0] = jnp.zeros((3 * ci, width), BF16)
        stacked[a, rows + 1] = jnp.zeros((3 * ci, width), BF16)

    def clear(a):
        def one(r):
            xp[a, r] = jnp.zeros((ci, width), BF16)
            gp[a, 1 + r] = jnp.zeros((co, width), BF16)

        copy_rows(rows, one)

    pl.when(s == 0)(lambda: clear(0))
    pl.when(s == ns - 1)(lambda: clear(2))

    landed(x_slot, xp.at[1, pl.ds((1 - y) * x_rows, x_rows)], "cout", 1 - y)
    x_up, go = link(xp.at[1], xp.at[0], "sp", s + 1, s < ns - 1)
    go()
    x_down, go = link(xp.at[1], xp.at[2], "sp", s - 1, s > 0)
    go()
    gather_wait(1)
    gather_send(2)

    def stack(a):
        def one(r):
            row = xp[a, r]
            for c in range(3):
                stacked[a, r + 1, pl.ds(c * ci, ci)] = shifted(row, c - 1)

        copy_rows(rows, one)

    stack(1)
    gather_wait(2)
    gather_send(3)
    landed(x_up, xp.at[0], "sp", s - 1, s > 0)
    stack(0)
    landed(x_down, xp.at[2], "sp", s + 1, s < ns - 1)
    stack(2)

    taps = [(a, b) for a in range(3) for b in range(3)]

    def output_chunk(index):
        def pair(step, carry):
            r = index * g_rows + step * 2
            total = None
            for group in (taps[0:4], taps[4:8], taps[8:9]):
                left = jnp.concatenate([kernel_t[a * 3 + b] for a, b in group], axis=1)
                right = jnp.concatenate(
                    [
                        jnp.concatenate([stacked[a, r + b], stacked[a, r + b + 1]], axis=1)
                        for a, b in group
                    ],
                    axis=0,
                )
                term = jnp.dot(left, right, preferred_element_type=F32)
                total = term if total is None else total + term
            op[r] = total[:, :width]
            op[r + 1] = total[:, width:]
            return carry

        lax.fori_loop(0, g_rows // 2, pair, 0)

    def chunk(index):
        return op.at[pl.ds(index * g_rows, g_rows)]

    def add_chunk(index, source):
        def one(r):
            op[index * g_rows + r] = op[index * g_rows + r] + source[r]

        copy_rows(g_rows, one)

    o_up, o_down = [], []

    def scatter_wait(t):
        landed(o_up[t], o_recv.at[0, t], "cin", z - 1, (z >= 1) & (z - 1 <= t))
        landed(o_down[t], o_recv.at[1, t], "cin", z + 1, (z <= nz - 2) & (nz - 2 - z <= t))

    def scatter_send(t):
        up_index, down_index = nz - 1 - t + z, t - (nz - 1) + z
        if t > 0:
            scatter_wait(t - 1)
            pl.when((z >= 1) & (z <= t) & (z < nz - 1))(
                lambda: add_chunk(up_index, o_recv.at[0, t - 1]))
            pl.when((z <= nz - 2) & (nz - 1 - z <= t) & (z > 0))(
                lambda: add_chunk(down_index, o_recv.at[1, t - 1]))
        slot, go = link(chunk(up_index), o_recv.at[0, t], "cin", z + 1, (z <= t) & (z < nz - 1))
        go()
        o_up.append(slot)
        slot, go = link(chunk(down_index), o_recv.at[1, t], "cin", z - 1, (nz - 1 - z <= t) & (z > 0))
        go()
        o_down.append(slot)

    low = z < 2
    order = [
        jnp.where(low, 3, 0),
        jnp.where(low, 2, 1),
        jnp.where(z == 0, 1, jnp.where(z == 1, 0, jnp.where(z == 2, 3, 2))),
        z,
    ]
    output_chunk(order[0])
    scatter_send(0)
    gather_wait(3)
    g_inner = pl.ds(1, rows)
    g_up, go = link(gp.at[1, g_inner], gp.at[0, g_inner], "sp", s + 1, s < ns - 1)
    go()
    g_down, go = link(gp.at[1, g_inner], gp.at[2, g_inner], "sp", s - 1, s > 0)
    go()
    output_chunk(order[1])
    output_chunk(order[2])
    output_chunk(order[3])

    def turn(r):
        turned[r] = gp[1, 1 + r].T

    copy_rows(rows, turn)
    span = 8
    part_rows = ci // 4

    def weight_plane(a):
        def tap(b):
            total = None
            for k in range(rows // span):
                left = jnp.concatenate(
                    [stacked[a, b + k * span + j] for j in range(span)], axis=1)
                right = jnp.concatenate([turned[k * span + j] for j in range(span)], axis=0)
                term = jnp.dot(left, right, preferred_element_type=F32)
                total = term if total is None else total + term
            for c in range(3):
                for q in range(4):
                    at = c * ci + q * part_rows
                    dwp[q, (a * 3 + b) * 3 + c] = total[at : at + part_rows]

        copy_rows(3, tap)

    first, second = [], []
    own = 2 * b0 + b1

    def halve(a):
        nine = pl.ds(9 * a, 9)
        slot, go = link(
            dwp.at[pl.ds(2 * (1 - b0), 2), nine], dw_half.at[:, nine], "sp", s + 1 - 2 * b0)
        go()
        first.append(slot)

    def quarter(a):
        nine = pl.ds(9 * a, 9)
        landed(first[a], dw_half.at[:, nine], "sp", s + 1 - 2 * b0)

        def add(k):
            for h in range(2):
                dwp[2 * b0 + h, 9 * a + k] = dwp[2 * b0 + h, 9 * a + k] + dw_half[h, 9 * a + k]

        copy_rows(9, add)
        slot, go = link(
            dwp.at[2 * b0 + 1 - b1, nine], dw_quarter.at[nine], "sp", (s + 2) % 4)
        go()
        second.append(slot)

    weight_plane(0)
    halve(0)
    scatter_send(1)
    weight_plane(1)
    halve(1)
    quarter(0)
    weight_plane(2)
    halve(2)
    quarter(1)

    landed(g_up, gp.at[0, g_inner], "sp", s - 1, s > 0)
    landed(g_down, gp.at[2, g_inner], "sp", s + 1, s < ns - 1)
    dx_rows = x_rows // 2

    def input_rows(begin, count):
        def pair(step, carry):
            r = begin + step * 2
            total = None
            for a in range(3):
                left = jnp.concatenate([kernel[a * 3 + b] for b in range(3)], axis=1)
                right = jnp.concatenate(
                    [
                        jnp.concatenate([gp[2 - a, r + 2 - b], gp[2 - a, r + 3 - b]], axis=1)
                        for b in range(3)
                    ],
                    axis=0,
                )
                term = jnp.dot(left, right, preferred_element_type=F32)
                total = term if total is None else total + term
            for k in range(2):
                part = total[:, k * width : (k + 1) * width]
                lane = lax.broadcasted_iota(jnp.int32, (ci, width), 1)
                ahead = pltpu.roll(part[0:ci], width - 1, 1)
                behind = pltpu.roll(part[2 * ci : 3 * ci], 1, 1)
                dxp[r + k] = (
                    part[ci : 2 * ci]
                    + jnp.where(lane == width - 1, 0.0, ahead)
                    + jnp.where(lane == 0, 0.0, behind)
                )
            return carry

        lax.fori_loop(0, count // 2, pair, 0)

    dx_slots = []
    for k in range(2):
        begin = (1 - y) * x_rows + k * dx_rows
        input_rows(begin, dx_rows)
        slot, go = link(
            dxp.at[pl.ds(begin, dx_rows)], dx_recv.at[pl.ds(k * dx_rows, dx_rows)], "cout", 1 - y)
        go()
        dx_slots.append(slot)
        if k == 0:
            quarter(2)
    scatter_send(2)
    input_rows(y * x_rows, x_rows)

    scale = 1.0 / math.sqrt(ns * rows * width)
    third = []
    for a in range(3):
        nine = pl.ds(9 * a, 9)
        landed(second[a], dw_quarter.at[nine], "sp", (s + 2) % 4)

        def finish(k, a=a):
            total = dwp[own, 9 * a + k] + dw_quarter[9 * a + k]
            dwb[own, 9 * a + k] = (total * scale).astype(BF16)

        copy_rows(9, finish)
        slot, go = link(dwb.at[own, nine], dwb.at[own, nine], "sp", (s + 2) % 4)
        go()
        third.append(slot)
    mine, theirs = pl.ds(2 * b0, 2), pl.ds(2 * (1 - b0), 2)
    fourth = []
    for a in range(3):
        nine = pl.ds(9 * a, 9)
        landed(third[a], dwb.at[2 * b0 + 1 - b1, nine], "sp", (s + 2) % 4)
        slot, go = link(dwb.at[mine, nine], dwb.at[mine, nine], "sp", s + 1 - 2 * b0)
        go()
        fourth.append(slot)

    for k in range(2):
        landed(dx_slots[k], dx_recv.at[pl.ds(k * dx_rows, dx_rows)], "cout", 1 - y)

    def put_dx(r):
        dx_out[r] = (dxp[y * x_rows + r] + dx_recv[r]).astype(BF16)

    copy_rows(x_rows, put_dx)
    for a in range(3):
        landed(fourth[a], dwb.at[theirs, pl.ds(9 * a, 9)], "sp", s + 1 - 2 * b0)

    def put_dw(k):
        for q in range(4):
            dw_out[k, pl.ds(q * part_rows, part_rows)] = dwb[q, k]

    copy_rows(27, put_dw)
    scatter_wait(nz - 2)
    pl.when(z > 0)(lambda: add_chunk(z, o_recv.at[0, nz - 2]))
    pl.when(z < nz - 1)(lambda: add_chunk(z, o_recv.at[1, nz - 2]))

    def put_out(r):
        out[r] = op[z * g_rows + r].astype(BF16)

    copy_rows(g_rows, put_out)
    for copy, when in sent:
        if when is None:
            copy.wait_send()
        else:
            pl.when(when)(copy.wait_send)


def whole(x_rows, g_rows, weights):
    ci, co = weights.shape[3:]
    half, _, width = x_rows.shape
    rows = 2 * half
    quarter = rows // 4
    kernel = weights.reshape(9, 3 * ci, co)
    transfers = 31
    return pl.pallas_call(
        whole_kernel,
        out_shape=[
            jax.ShapeDtypeStruct((quarter, co, width), BF16),
            jax.ShapeDtypeStruct((half, ci, width), BF16),
            jax.ShapeDtypeStruct((27, ci, co), BF16),
        ],
        in_specs=[pl.BlockSpec(memory_space=pltpu.VMEM)] * 4,
        out_specs=[pl.BlockSpec(memory_space=pltpu.VMEM)] * 3,
        scratch_shapes=[
            pltpu.VMEM((3, rows, ci, width), BF16),
            pltpu.VMEM((3, rows + 2, 3 * ci, width), BF16),
            pltpu.VMEM((3, rows + 2, co, width), BF16),
            pltpu.VMEM((rows, width, co), BF16),
            pltpu.VMEM((rows, co, width), F32),
            pltpu.VMEM((2, 3, quarter, co, width), F32),
            pltpu.VMEM((4, 27, ci // 4, co), F32),
            pltpu.VMEM((2, 27, ci // 4, co), F32),
            pltpu.VMEM((27, ci // 4, co), F32),
            pltpu.VMEM((4, 27, ci // 4, co), BF16),
            pltpu.VMEM((rows, ci, width), F32),
            pltpu.VMEM((half, ci, width), F32),
            pltpu.SemaphoreType.DMA((transfers,)),
            pltpu.SemaphoreType.DMA((transfers,)),
        ],
        compiler_params=pltpu.CompilerParams(
            collective_id=0, has_side_effects=True, vmem_limit_bytes=60 * 1024 * 1024
        ),
        cost_estimate=pl.CostEstimate(
            flops=6 * 27 * ci * co * rows * width, bytes_accessed=8 << 20, transcendentals=0
        ),
    )(x_rows, g_rows, kernel.transpose(0, 2, 1), kernel)


def body(activations, weights, out_grad):
    grad_rows = out_grad[:, 0].transpose(1, 0, 2)
    x_rows = activations[:, 0].transpose(1, 0, 2)
    counts = tuple(lax.axis_size(axis) for axis in ("cin", "cout", "sp"))
    if counts == (4, 2, 4) and weights.shape[3] % 128 == 0 and weights.shape[4] % 128 == 0:
        output, in_grad, weight_grad = whole(x_rows, grad_rows, weights)
        return (
            output.transpose(1, 0, 2)[:, None],
            in_grad.transpose(1, 0, 2)[:, None],
            weight_grad.reshape(weights.shape),
        )
    x_panel = line_gather(x_rows, "cout")
    g_panel = line_gather(grad_rows, "cin")
    x_planes = with_neighbours(x_panel)
    g_planes = with_neighbours(g_panel)
    partial_out = local_output(x_planes, weights)
    output = line_reduce_scatter(partial_out, "cin")
    output = output.transpose(1, 0, 2).astype(BF16)[:, None]
    partial_weights = local_weight_grad(x_planes, g_panel)
    voxels = lax.axis_size("sp") * g_panel.shape[0] * g_panel.shape[2]
    weight_grad = reduce_all(partial_weights, "sp", 1.0 / math.sqrt(voxels))
    partial_in = local_input_grad(g_planes, weights)
    in_grad = line_reduce_scatter(partial_in, "cout")
    in_grad = in_grad.transpose(1, 0, 2).astype(BF16)[:, None]
    return (output, in_grad, weight_grad.reshape(weights.shape))


def solution(mesh):
    return jax.shard_map(
        body,
        mesh=mesh,
        in_specs=(
            P("cin", "sp", "cout", None),
            P(None, None, None, "cin", "cout"),
            P("cout", "sp", "cin", None),
        ),
        out_specs=(
            P("cout", "sp", "cin", None),
            P("cin", "sp", "cout", None),
            P(None, None, None, "cin", "cout"),
        ),
        check_vma=False,
    )
```

```python
import functools
import math

import jax
import jax.numpy as jnp
from jax import lax
from jax.experimental import pallas as pl
from jax.experimental.pallas import tpu as pltpu
from jax.sharding import PartitionSpec as P

F32 = jnp.float32
BF16 = jnp.bfloat16
VMEM_BYTES = 56 * 1024 * 1024


def right_pairs(first, last):
    return [(i, i + 1) for i in range(first, last)]


def left_pairs(first, last):
    return [(i + 1, i) for i in range(first, last)]


def line_gather(block, axis):
    count = lax.axis_size(axis)
    from_low, from_high = [], []
    moving_up, moving_down = block, block
    for step in range(1, count):
        moving_up = lax.ppermute(moving_up, axis, right_pairs(step - 1, count - 1))
        moving_down = lax.ppermute(moving_down, axis, left_pairs(0, count - step))
        from_low.insert(0, moving_up)
        from_high.append(moving_down)
    if count == 2:
        low, high = from_low[0], from_high[0]
        first = lax.axis_index(axis) == 0
        return jnp.concatenate(
            [jnp.where(first, block, low), jnp.where(first, high, block)], axis=0
        )
    around = jnp.concatenate(from_low + [block] + from_high, axis=0)
    extent = block.shape[0]
    start = (count - 1 - lax.axis_index(axis)) * extent
    return lax.dynamic_slice_in_dim(around, start, count * extent, axis=0)


def line_reduce_scatter(partial, axis):
    count = lax.axis_size(axis)
    me = lax.axis_index(axis)
    extent = partial.shape[0] // count

    def chunk(index):
        index = jnp.clip(index, 0, count - 1)
        return lax.dynamic_slice_in_dim(partial, index * extent, extent, axis=0)

    up, down = None, None
    for step in range(count - 1):
        send_up = chunk(count - 1 - step + me)
        send_down = chunk(step - (count - 1) + me)
        if up is not None:
            send_up = send_up + up
            send_down = send_down + down
        up = lax.ppermute(send_up, axis, right_pairs(0, step + 1))
        down = lax.ppermute(send_down, axis, left_pairs(count - 2 - step, count - 1))
    return chunk(me) + up + down


def exchange(value, axis, distance):
    count = lax.axis_size(axis)
    return lax.ppermute(value, axis, [(i, i ^ distance) for i in range(count)])


def reduce_all(partial, axis, scale):
    count = lax.axis_size(axis)
    me = lax.axis_index(axis)
    held = partial
    distance = 1
    while distance < count:
        half = held.shape[1] // 2
        bit = (me // distance) % 2
        mine = lax.dynamic_slice_in_dim(held, bit * half, half, axis=1)
        other = lax.dynamic_slice_in_dim(held, (1 - bit) * half, half, axis=1)
        held = mine + exchange(other, axis, distance)
        distance *= 2
    held = (held * scale).astype(BF16)
    while distance > 1:
        distance //= 2
        bit = (me // distance) % 2
        other = exchange(held, axis, distance)
        low = jnp.where(bit == 0, held, other)
        high = jnp.where(bit == 0, other, held)
        held = jnp.concatenate([low, high], axis=1)
    return held


def shifted(row, offset):
    if offset == 0:
        return row
    width = row.shape[1]
    wide = pltpu.roll(row.astype(F32), (-offset) % width, 1)
    lane = lax.broadcasted_iota(jnp.int32, wide.shape, 1)
    edge = width - 1 if offset > 0 else 0
    return jnp.where(lane == edge, 0.0, wide).astype(row.dtype)


def stack_shifts(planes, stacked):
    rows, channels, width = planes[0].shape
    for a, plane in enumerate(planes):
        stacked[a, 0] = jnp.zeros((3 * channels, width), BF16)
        stacked[a, rows + 1] = jnp.zeros((3 * channels, width), BF16)

        def one(r, carry, a=a, plane=plane):
            row = plane[r]
            for c in range(3):
                stacked[a, r + 1, pl.ds(c * channels, channels)] = shifted(row, c - 1)
            return carry

        lax.fori_loop(0, rows, one, 0)


def output_kernel(low, mid, high, kernel, out, stacked):
    stack_shifts((low, mid, high), stacked)
    taps = [(a, b) for a in range(3) for b in range(3)]

    def pair(step, carry):
        r = step * 2
        total = None
        for group in (taps[0:4], taps[4:8], taps[8:9]):
            left = jnp.concatenate([kernel[a * 3 + b] for a, b in group], axis=1)
            right = jnp.concatenate(
                [
                    jnp.concatenate([stacked[a, r + b], stacked[a, r + b + 1]], axis=1)
                    for a, b in group
                ],
                axis=0,
            )
            term = jnp.dot(left, right, preferred_element_type=F32)
            total = term if total is None else total + term
        width = mid.shape[2]
        out[r] = total[:, :width]
        out[r + 1] = total[:, width:]
        return carry

    lax.fori_loop(0, mid.shape[0] // 2, pair, 0)


def input_grad_kernel(low, mid, high, kernel, out, padded):
    rows, channels, width = mid.shape
    for a, plane in enumerate((low, mid, high)):
        padded[a, 0] = jnp.zeros((channels, width), BF16)
        padded[a, rows + 1] = jnp.zeros((channels, width), BF16)

        def one(r, carry, a=a, plane=plane):
            padded[a, r + 1] = plane[r]
            return carry

        lax.fori_loop(0, rows, one, 0)
    inner = out.shape[1]

    def pair(step, carry):
        r = step * 2
        total = None
        for a in range(3):
            left = jnp.concatenate([kernel[a * 3 + b] for b in range(3)], axis=1)
            right = jnp.concatenate(
                [
                    jnp.concatenate([padded[2 - a, r + 2 - b], padded[2 - a, r + 3 - b]], axis=1)
                    for b in range(3)
                ],
                axis=0,
            )
            term = jnp.dot(left, right, preferred_element_type=F32)
            total = term if total is None else total + term
        for k in range(2):
            part = total[:, k * width : (k + 1) * width]
            lane = lax.broadcasted_iota(jnp.int32, (inner, width), 1)
            ahead = pltpu.roll(part[0:inner], width - 1, 1)
            behind = pltpu.roll(part[2 * inner : 3 * inner], 1, 1)
            out[r + k] = (
                part[inner : 2 * inner]
                + jnp.where(lane == width - 1, 0.0, ahead)
                + jnp.where(lane == 0, 0.0, behind)
            )
        return carry

    lax.fori_loop(0, rows // 2, pair, 0)


def weight_grad_kernel(low, mid, high, grad, out, stacked, turned):
    rows = mid.shape[0]
    stack_shifts((low, mid, high), stacked)

    def turn(r, carry):
        turned[r] = grad[r].T
        return carry

    lax.fori_loop(0, rows, turn, 0)
    span = 8

    for a in range(3):

        def tap(b, carry, a=a):
            def part(k):
                left = jnp.concatenate(
                    [stacked[a, b + k * span + j] for j in range(span)], axis=1
                )
                right = jnp.concatenate([turned[k * span + j] for j in range(span)], axis=0)
                return jnp.dot(left, right, preferred_element_type=F32)

            total = part(0)
            for k in range(1, rows // span):
                total = total + part(k)
            out[a * 3 + b] = total
            return carry

        lax.fori_loop(0, 3, tap, 0)


def call(kernel, operands, out_shape, scratch):
    flops = 2 * 27 * 128 * 256 * 4096
    return pl.pallas_call(
        kernel,
        out_shape=jax.ShapeDtypeStruct(out_shape, F32),
        in_specs=[pl.BlockSpec(memory_space=pltpu.VMEM)] * len(operands),
        out_specs=pl.BlockSpec(memory_space=pltpu.VMEM),
        scratch_shapes=[pltpu.VMEM(shape, BF16) for shape in scratch],
        compiler_params=pltpu.CompilerParams(vmem_limit_bytes=VMEM_BYTES),
        cost_estimate=pl.CostEstimate(flops=flops, bytes_accessed=8 << 20, transcendentals=0),
    )(*operands)


def plain_conv(planes, kernel):
    return lax.conv_general_dilated(
        planes.transpose(2, 0, 1, 3)[None],
        kernel,
        (1, 1, 1),
        [(0, 0), (1, 1), (1, 1)],
        dimension_numbers=("NCDHW", "DHWIO", "NCDHW"),
        preferred_element_type=F32,
    )[0, :, 0].transpose(1, 0, 2)


def local_output(planes, weights):
    ci, co = weights.shape[3:]
    rows, _, width = planes[1].shape
    if ci % 128 or co % 128:
        return plain_conv(jnp.stack(planes), weights)
    kernel = weights.reshape(9, 3 * ci, co).transpose(0, 2, 1)
    return call(
        output_kernel, (*planes, kernel), (rows, co, width), [(3, rows + 2, 3 * ci, width)]
    )


def local_input_grad(planes, weights):
    ci, co = weights.shape[3:]
    rows, _, width = planes[1].shape
    if ci % 128 or co % 128:
        flipped = jnp.transpose(weights[::-1, ::-1, ::-1], (0, 1, 2, 4, 3))
        return plain_conv(jnp.stack(planes), flipped)
    kernel = weights.reshape(9, 3 * ci, co)
    return call(
        input_grad_kernel, (*planes, kernel), (rows, ci, width), [(3, rows + 2, co, width)]
    )


def local_weight_grad(planes, grad):
    rows, ci, width = planes[1].shape
    co = grad.shape[1]
    if ci % 128 or co % 128:
        padded = jnp.pad(jnp.stack(planes), ((0, 0), (1, 1), (0, 0), (1, 1)))
        terms = [
            jnp.einsum(
                "rcw,row->co",
                padded[a, b : b + rows, :, c : c + width],
                grad,
                preferred_element_type=F32,
            )
            for a in range(3)
            for b in range(3)
            for c in range(3)
        ]
        return jnp.stack(terms)
    out = call(
        weight_grad_kernel,
        (*planes, grad),
        (9, 3 * ci, co),
        [(3, rows + 2, 3 * ci, width), (rows, width, co)],
    )
    return out.reshape(27, ci, co)


def with_neighbours(plane):
    count = lax.axis_size("sp")
    low = lax.ppermute(plane, "sp", right_pairs(0, count - 1))
    high = lax.ppermute(plane, "sp", left_pairs(0, count - 1))
    return low, plane, high


def whole_kernel(
    x_own, g_own, kernel, out, dx_out, dw_out,
    kernel_t, wide, xp, stacked, gp, turned, op, o_recv, dwp, dw_half, dw_quarter, dwb, dxp, dx_recv, send, recv,
):
    z, y, s = lax.axis_index("cin"), lax.axis_index("cout"), lax.axis_index("sp")
    nz, ns = 4, 4
    rows, ci, width = xp.shape[1:]
    co = gp.shape[2]
    g_rows, x_rows = rows // nz, rows // 2
    b0, b1 = s % 2, s // 2
    used = [0]
    sent = []

    def link(src, dst, axis, target, when=None):
        slot = used[0]
        used[0] += 1
        copy = pltpu.make_async_remote_copy(
            src_ref=src, dst_ref=dst, send_sem=send.at[slot], recv_sem=recv.at[slot],
            device_id={axis: target}, device_id_type=pl.DeviceIdType.MESH,
        )

        def start():
            if when is None:
                copy.start()
            else:
                pl.when(when)(copy.start)

        sent.append((copy, when))
        return slot, start

    def landed(slot, dst, axis, target, when=None):
        copy = pltpu.make_async_remote_copy(
            src_ref=dst, dst_ref=dst, send_sem=send.at[slot], recv_sem=recv.at[slot],
            device_id={axis: target}, device_id_type=pl.DeviceIdType.MESH,
        )
        if when is None:
            copy.wait_recv()
        else:
            pl.when(when)(copy.wait_recv)

    partners = [
        ("cin", z - 1, z > 0), ("cin", z + 1, z < nz - 1), ("cout", 1 - y, None),
        ("sp", s - 1, s > 0), ("sp", s + 1, s < ns - 1), ("sp", (s + 2) % 4, None),
    ]
    barrier = pltpu.get_barrier_semaphore()

    def each(action):
        for axis, target, when in partners:
            if when is None:
                action(axis, target)
            else:
                pl.when(when)(functools.partial(action, axis, target))

    each(lambda axis, target: pl.semaphore_signal(
        barrier, inc=1, device_id={axis: target}, device_id_type=pl.DeviceIdType.MESH))
    peers = 2
    for inside in (z > 0, z < nz - 1, s > 0, s < ns - 1):
        peers = peers + jnp.where(inside, 1, 0)
    pl.semaphore_wait(barrier, peers)

    def copy_rows(count, store):
        def one(r, carry):
            store(r)
            return carry

        lax.fori_loop(0, count, one, 0)

    flat = wide.shape[0] // 16

    def widen(source):
        def one(k):
            at = pl.ds(k * flat, flat)
            wide[at] = source[at].astype(F32)

        copy_rows(16, one)

    def narrow(target):
        def one(k):
            at = pl.ds(k * flat, flat)
            target[at] = wide[at].astype(BF16)

        copy_rows(16, one)

    def put_g(r):
        gp[1, 1 + z * g_rows + r] = wide[pl.ds(r, co, stride=g_rows)].astype(BF16)

    def put_x(r):
        xp[1, y * x_rows + r] = wide[pl.ds(r, ci, stride=x_rows)].astype(BF16)

    mine_x, theirs_x = pl.ds(y * x_rows, x_rows), pl.ds((1 - y) * x_rows, x_rows)
    widen(x_own)
    copy_rows(x_rows, put_x)
    x_slot, go = link(xp.at[1, mine_x], xp.at[1, mine_x], "cout", 1 - y)
    go()

    def depth_send(part):
        up, go = link(xp.at[1, part], xp.at[0, part], "sp", s + 1, s < ns - 1)
        go()
        down, go = link(xp.at[1, part], xp.at[2, part], "sp", s - 1, s > 0)
        go()
        return up, down

    def depth_wait(slots, part):
        landed(slots[0], xp.at[0, part], "sp", s - 1, s > 0)
        landed(slots[1], xp.at[2, part], "sp", s + 1, s < ns - 1)

    mine_slots = depth_send(mine_x)
    widen(g_own)
    copy_rows(g_rows, put_g)

    def g_block(index):
        return gp.at[1, pl.ds(1 + index * g_rows, g_rows)]

    up_slots, down_slots = [], []

    def gather_send(t):
        up_source = g_block(z - (t - 1))
        slot, go = link(up_source, g_block(z - (t - 1)), "cin", z + 1, (z >= t - 1) & (z < nz - 1))
        go()
        up_slots.append(slot)
        down_source = g_block(z + (t - 1))
        slot, go = link(down_source, g_block(z + (t - 1)), "cin", z - 1, (z <= nz - t) & (z > 0))
        go()
        down_slots.append(slot)

    def gather_wait(t):
        landed(up_slots[t - 1], g_block(z - t), "cin", z - 1, z >= t)
        landed(down_slots[t - 1], g_block(z + t), "cin", z + 1, z <= nz - 1 - t)

    gather_send(1)
    for a in range(3):
        gp[a, 0] = jnp.zeros((co, width), BF16)
        gp[a, rows + 1] = jnp.zeros((co, width), BF16)
        stacked[a, 0] = jnp.zeros((3 * ci, width), BF16)
        stacked[a, rows + 1] = jnp.zeros((3 * ci, width), BF16)

    def clear(a):
        def one(r):
            xp[a, r] = jnp.zeros((ci, width), BF16)
            gp[a, 1 + r] = jnp.zeros((co, width), BF16)

        copy_rows(rows, one)

    pl.when(s == 0)(lambda: clear(0))
    pl.when(s == ns - 1)(lambda: clear(2))

    def turn_kernel(k):
        kernel_t[k] = kernel[k].T

    def stack(a, half):
        def one(r):
            row = xp[a, half * x_rows + r]
            for c in range(3):
                stacked[a, half * x_rows + r + 1, pl.ds(c * ci, ci)] = shifted(row, c - 1)

        copy_rows(x_rows, one)

    stack(1, y)
    copy_rows(9, turn_kernel)
    depth_wait(mine_slots, mine_x)
    stack(0, y)
    stack(2, y)
    landed(x_slot, xp.at[1, theirs_x], "cout", 1 - y)
    theirs_slots = depth_send(theirs_x)
    gather_wait(1)
    gather_send(2)
    stack(1, 1 - y)
    depth_wait(theirs_slots, theirs_x)
    stack(0, 1 - y)
    stack(2, 1 - y)

    taps = [(a, b) for a in range(3) for b in range(3)]

    def output_chunk(index):
        def pair(step, carry):
            r = index * g_rows + step * 2
            total = None
            for group in (taps[0:4], taps[4:8], taps[8:9]):
                left = jnp.concatenate([kernel_t[a * 3 + b] for a, b in group], axis=1)
                right = jnp.concatenate(
                    [
                        jnp.concatenate([stacked[a, r + b], stacked[a, r + b + 1]], axis=1)
                        for a, b in group
                    ],
                    axis=0,
                )
                term = jnp.dot(left, right, preferred_element_type=F32)
                total = term if total is None else total + term
            op[r] = total[:, :width]
            op[r + 1] = total[:, width:]
            return carry

        lax.fori_loop(0, g_rows // 2, pair, 0)

    def chunk(index):
        return op.at[pl.ds(index * g_rows, g_rows)]

    def add_chunk(index, source):
        def one(r):
            op[index * g_rows + r] = op[index * g_rows + r] + source[r]

        copy_rows(g_rows, one)

    o_up, o_down = [], []

    def scatter_wait(t):
        landed(o_up[t], o_recv.at[0, t], "cin", z - 1, (z >= 1) & (z - 1 <= t))
        landed(o_down[t], o_recv.at[1, t], "cin", z + 1, (z <= nz - 2) & (nz - 2 - z <= t))

    def scatter_send(t):
        up_index, down_index = nz - 1 - t + z, t - (nz - 1) + z
        if t > 0:
            scatter_wait(t - 1)
            pl.when((z >= 1) & (z <= t) & (z < nz - 1))(
                lambda: add_chunk(up_index, o_recv.at[0, t - 1]))
            pl.when((z <= nz - 2) & (nz - 1 - z <= t) & (z > 0))(
                lambda: add_chunk(down_index, o_recv.at[1, t - 1]))
        slot, go = link(chunk(up_index), o_recv.at[0, t], "cin", z + 1, (z <= t) & (z < nz - 1))
        go()
        o_up.append(slot)
        slot, go = link(chunk(down_index), o_recv.at[1, t], "cin", z - 1, (nz - 1 - z <= t) & (z > 0))
        go()
        o_down.append(slot)

    low = z < 2
    order = [
        jnp.where(low, 3, 0),
        jnp.where(low, 2, 1),
        jnp.where(z == 0, 1, jnp.where(z == 1, 0, jnp.where(z == 2, 3, 2))),
        z,
    ]
    output_chunk(order[0])
    scatter_send(0)
    gather_wait(2)
    gather_send(3)
    output_chunk(order[1])
    output_chunk(order[2])
    gather_wait(3)
    g_inner = pl.ds(1, rows)
    g_up, go = link(gp.at[1, g_inner], gp.at[0, g_inner], "sp", s + 1, s < ns - 1)
    go()
    g_down, go = link(gp.at[1, g_inner], gp.at[2, g_inner], "sp", s - 1, s > 0)
    go()
    output_chunk(order[3])

    def turn(r):
        turned[r] = gp[1, 1 + r].T

    copy_rows(rows, turn)
    span = 8
    part_rows = ci // 4

    def weight_plane(a):
        def tap(b):
            total = None
            for k in range(rows // span):
                left = jnp.concatenate(
                    [stacked[a, b + k * span + j] for j in range(span)], axis=1)
                right = jnp.concatenate([turned[k * span + j] for j in range(span)], axis=0)
                term = jnp.dot(left, right, preferred_element_type=F32)
                total = term if total is None else total + term
            for c in range(3):
                for q in range(4):
                    at = c * ci + q * part_rows
                    dwp[q, (a * 3 + b) * 3 + c] = total[at : at + part_rows]

        copy_rows(3, tap)

    first, second = [], []
    own = 2 * b0 + b1

    def halve(a):
        nine = pl.ds(9 * a, 9)
        slot, go = link(
            dwp.at[pl.ds(2 * (1 - b0), 2), nine], dw_half.at[:, nine], "sp", s + 1 - 2 * b0)
        go()
        first.append(slot)

    def quarter(a):
        nine = pl.ds(9 * a, 9)
        landed(first[a], dw_half.at[:, nine], "sp", s + 1 - 2 * b0)

        def add(k):
            for h in range(2):
                dwp[2 * b0 + h, 9 * a + k] = dwp[2 * b0 + h, 9 * a + k] + dw_half[h, 9 * a + k]

        copy_rows(9, add)
        slot, go = link(
            dwp.at[2 * b0 + 1 - b1, nine], dw_quarter.at[nine], "sp", (s + 2) % 4)
        go()
        second.append(slot)

    weight_plane(0)
    halve(0)
    scatter_send(1)
    weight_plane(1)
    halve(1)
    quarter(0)
    weight_plane(2)
    halve(2)
    quarter(1)

    landed(g_up, gp.at[0, g_inner], "sp", s - 1, s > 0)
    landed(g_down, gp.at[2, g_inner], "sp", s + 1, s < ns - 1)
    dx_rows = x_rows // 2

    def input_rows(begin, count):
        def pair(step, carry):
            r = begin + step * 2
            total = None
            for a in range(3):
                left = jnp.concatenate([kernel[a * 3 + b] for b in range(3)], axis=1)
                right = jnp.concatenate(
                    [
                        jnp.concatenate([gp[2 - a, r + 2 - b], gp[2 - a, r + 3 - b]], axis=1)
                        for b in range(3)
                    ],
                    axis=0,
                )
                term = jnp.dot(left, right, preferred_element_type=F32)
                total = term if total is None else total + term
            for k in range(2):
                part = total[:, k * width : (k + 1) * width]
                lane = lax.broadcasted_iota(jnp.int32, (ci, width), 1)
                ahead = pltpu.roll(part[0:ci], width - 1, 1)
                behind = pltpu.roll(part[2 * ci : 3 * ci], 1, 1)
                dxp[r + k] = (
                    part[ci : 2 * ci]
                    + jnp.where(lane == width - 1, 0.0, ahead)
                    + jnp.where(lane == 0, 0.0, behind)
                )
            return carry

        lax.fori_loop(0, count // 2, pair, 0)

    dx_slots = []
    for k in range(2):
        begin = (1 - y) * x_rows + k * dx_rows
        input_rows(begin, dx_rows)
        slot, go = link(
            dxp.at[pl.ds(begin, dx_rows)], dx_recv.at[pl.ds(k * dx_rows, dx_rows)], "cout", 1 - y)
        go()
        dx_slots.append(slot)
        if k == 0:
            quarter(2)
    scatter_send(2)
    input_rows(y * x_rows, x_rows)

    scale = 1.0 / math.sqrt(ns * rows * width)
    third = []
    for a in range(3):
        nine = pl.ds(9 * a, 9)
        landed(second[a], dw_quarter.at[nine], "sp", (s + 2) % 4)

        def finish(k, a=a):
            total = dwp[own, 9 * a + k] + dw_quarter[9 * a + k]
            dwb[own, 9 * a + k] = (total * scale).astype(BF16)

        copy_rows(9, finish)
        slot, go = link(dwb.at[own, nine], dwb.at[own, nine], "sp", (s + 2) % 4)
        go()
        third.append(slot)
    mine, theirs = pl.ds(2 * b0, 2), pl.ds(2 * (1 - b0), 2)
    fourth = []
    for a in range(3):
        nine = pl.ds(9 * a, 9)
        landed(third[a], dwb.at[2 * b0 + 1 - b1, nine], "sp", (s + 2) % 4)
        slot, go = link(dwb.at[mine, nine], dwb.at[mine, nine], "sp", s + 1 - 2 * b0)
        go()
        fourth.append(slot)

    for k in range(2):
        landed(dx_slots[k], dx_recv.at[pl.ds(k * dx_rows, dx_rows)], "cout", 1 - y)

    def put_dx(r):
        wide[pl.ds(r, ci, stride=x_rows)] = dxp[y * x_rows + r] + dx_recv[r]

    copy_rows(x_rows, put_dx)
    narrow(dx_out)
    for a in range(3):
        landed(fourth[a], dwb.at[theirs, pl.ds(9 * a, 9)], "sp", s + 1 - 2 * b0)

    def put_dw(k):
        for q in range(4):
            dw_out[k, pl.ds(q * part_rows, part_rows)] = dwb[q, k]

    copy_rows(27, put_dw)
    scatter_wait(nz - 2)
    def put_out(directions):
        def one(r):
            total = op[z * g_rows + r]
            for way in directions:
                total = total + o_recv[way, nz - 2, r]
            wide[pl.ds(r, co, stride=g_rows)] = total

        copy_rows(g_rows, one)

    pl.when(z == 0)(lambda: put_out((1,)))
    pl.when(z == nz - 1)(lambda: put_out((0,)))
    pl.when((z > 0) & (z < nz - 1))(lambda: put_out((0, 1)))
    narrow(out)
    for copy, when in sent:
        if when is None:
            copy.wait_send()
        else:
            pl.when(when)(copy.wait_send)


def whole(activations, out_grad, weights):
    ci, co = weights.shape[3:]
    half, width = activations.shape[2:]
    rows = 2 * half
    quarter = rows // 4
    kernel = weights.reshape(9, 3 * ci, co)
    transfers = 33
    return pl.pallas_call(
        whole_kernel,
        out_shape=[
            jax.ShapeDtypeStruct((co * quarter, width), BF16),
            jax.ShapeDtypeStruct((ci * half, width), BF16),
            jax.ShapeDtypeStruct((27, ci, co), BF16),
        ],
        in_specs=[pl.BlockSpec(memory_space=pltpu.VMEM)] * 3,
        out_specs=[pl.BlockSpec(memory_space=pltpu.VMEM)] * 3,
        scratch_shapes=[
            pltpu.VMEM((9, co, 3 * ci), BF16),
            pltpu.VMEM((ci * half, width), F32),
            pltpu.VMEM((3, rows, ci, width), BF16),
            pltpu.VMEM((3, rows + 2, 3 * ci, width), BF16),
            pltpu.VMEM((3, rows + 2, co, width), BF16),
            pltpu.VMEM((rows, width, co), BF16),
            pltpu.VMEM((rows, co, width), F32),
            pltpu.VMEM((2, 3, quarter, co, width), F32),
            pltpu.VMEM((4, 27, ci // 4, co), F32),
            pltpu.VMEM((2, 27, ci // 4, co), F32),
            pltpu.VMEM((27, ci // 4, co), F32),
            pltpu.VMEM((4, 27, ci // 4, co), BF16),
            pltpu.VMEM((rows, ci, width), F32),
            pltpu.VMEM((half, ci, width), F32),
            pltpu.SemaphoreType.DMA((transfers,)),
            pltpu.SemaphoreType.DMA((transfers,)),
        ],
        compiler_params=pltpu.CompilerParams(
            collective_id=0, has_side_effects=True, vmem_limit_bytes=60 * 1024 * 1024
        ),
        cost_estimate=pl.CostEstimate(
            flops=6 * 27 * ci * co * rows * width, bytes_accessed=8 << 20, transcendentals=0
        ),
    )(activations.reshape(ci * half, width), out_grad.reshape(co * quarter, width), kernel)


def body(activations, weights, out_grad):
    grad_rows = out_grad[:, 0].transpose(1, 0, 2)
    x_rows = activations[:, 0].transpose(1, 0, 2)
    counts = tuple(lax.axis_size(axis) for axis in ("cin", "cout", "sp"))
    lanes = weights.shape[3] % 128 == 0 and weights.shape[4] % 128 == 0
    if counts == (4, 2, 4) and lanes and weights.shape[4] == 2 * weights.shape[3]:
        output, in_grad, weight_grad = whole(activations, out_grad, weights)
        return (
            output.reshape(out_grad.shape),
            in_grad.reshape(activations.shape),
            weight_grad.reshape(weights.shape),
        )
    x_panel = line_gather(x_rows, "cout")
    g_panel = line_gather(grad_rows, "cin")
    x_planes = with_neighbours(x_panel)
    g_planes = with_neighbours(g_panel)
    partial_out = local_output(x_planes, weights)
    output = line_reduce_scatter(partial_out, "cin")
    output = output.transpose(1, 0, 2).astype(BF16)[:, None]
    partial_weights = local_weight_grad(x_planes, g_panel)
    voxels = lax.axis_size("sp") * g_panel.shape[0] * g_panel.shape[2]
    weight_grad = reduce_all(partial_weights, "sp", 1.0 / math.sqrt(voxels))
    partial_in = local_input_grad(g_planes, weights)
    in_grad = line_reduce_scatter(partial_in, "cout")
    in_grad = in_grad.transpose(1, 0, 2).astype(BF16)[:, None]
    return (output, in_grad, weight_grad.reshape(weights.shape))


def solution(mesh):
    return jax.shard_map(
        body,
        mesh=mesh,
        in_specs=(
            P("cin", "sp", "cout", None),
            P(None, None, None, "cin", "cout"),
            P("cout", "sp", "cin", None),
        ),
        out_specs=(
            P("cout", "sp", "cin", None),
            P("cin", "sp", "cout", None),
            P(None, None, None, "cin", "cout"),
        ),
        check_vma=False,
    )
```

```python
import functools
import math

import jax
import jax.numpy as jnp
from jax import lax
from jax.experimental import pallas as pl
from jax.experimental.pallas import tpu as pltpu
from jax.sharding import PartitionSpec as P

F32 = jnp.float32
BF16 = jnp.bfloat16
VMEM_BYTES = 56 * 1024 * 1024


def right_pairs(first, last):
    return [(i, i + 1) for i in range(first, last)]


def left_pairs(first, last):
    return [(i + 1, i) for i in range(first, last)]


def line_gather(block, axis):
    count = lax.axis_size(axis)
    from_low, from_high = [], []
    moving_up, moving_down = block, block
    for step in range(1, count):
        moving_up = lax.ppermute(moving_up, axis, right_pairs(step - 1, count - 1))
        moving_down = lax.ppermute(moving_down, axis, left_pairs(0, count - step))
        from_low.insert(0, moving_up)
        from_high.append(moving_down)
    if count == 2:
        low, high = from_low[0], from_high[0]
        first = lax.axis_index(axis) == 0
        return jnp.concatenate(
            [jnp.where(first, block, low), jnp.where(first, high, block)], axis=0
        )
    around = jnp.concatenate(from_low + [block] + from_high, axis=0)
    extent = block.shape[0]
    start = (count - 1 - lax.axis_index(axis)) * extent
    return lax.dynamic_slice_in_dim(around, start, count * extent, axis=0)


def line_reduce_scatter(partial, axis):
    count = lax.axis_size(axis)
    me = lax.axis_index(axis)
    extent = partial.shape[0] // count

    def chunk(index):
        index = jnp.clip(index, 0, count - 1)
        return lax.dynamic_slice_in_dim(partial, index * extent, extent, axis=0)

    up, down = None, None
    for step in range(count - 1):
        send_up = chunk(count - 1 - step + me)
        send_down = chunk(step - (count - 1) + me)
        if up is not None:
            send_up = send_up + up
            send_down = send_down + down
        up = lax.ppermute(send_up, axis, right_pairs(0, step + 1))
        down = lax.ppermute(send_down, axis, left_pairs(count - 2 - step, count - 1))
    return chunk(me) + up + down


def exchange(value, axis, distance):
    count = lax.axis_size(axis)
    return lax.ppermute(value, axis, [(i, i ^ distance) for i in range(count)])


def reduce_all(partial, axis, scale):
    count = lax.axis_size(axis)
    me = lax.axis_index(axis)
    held = partial
    distance = 1
    while distance < count:
        half = held.shape[1] // 2
        bit = (me // distance) % 2
        mine = lax.dynamic_slice_in_dim(held, bit * half, half, axis=1)
        other = lax.dynamic_slice_in_dim(held, (1 - bit) * half, half, axis=1)
        held = mine + exchange(other, axis, distance)
        distance *= 2
    held = (held * scale).astype(BF16)
    while distance > 1:
        distance //= 2
        bit = (me // distance) % 2
        other = exchange(held, axis, distance)
        low = jnp.where(bit == 0, held, other)
        high = jnp.where(bit == 0, other, held)
        held = jnp.concatenate([low, high], axis=1)
    return held


def shifted(row, offset):
    if offset == 0:
        return row
    width = row.shape[1]
    wide = pltpu.roll(row.astype(F32), (-offset) % width, 1)
    lane = lax.broadcasted_iota(jnp.int32, wide.shape, 1)
    edge = width - 1 if offset > 0 else 0
    return jnp.where(lane == edge, 0.0, wide).astype(row.dtype)


def stack_shifts(planes, stacked):
    rows, channels, width = planes[0].shape
    for a, plane in enumerate(planes):
        stacked[a, 0] = jnp.zeros((3 * channels, width), BF16)
        stacked[a, rows + 1] = jnp.zeros((3 * channels, width), BF16)

        def one(r, carry, a=a, plane=plane):
            row = plane[r]
            for c in range(3):
                stacked[a, r + 1, pl.ds(c * channels, channels)] = shifted(row, c - 1)
            return carry

        lax.fori_loop(0, rows, one, 0)


def output_kernel(low, mid, high, kernel, out, stacked):
    stack_shifts((low, mid, high), stacked)
    taps = [(a, b) for a in range(3) for b in range(3)]

    def pair(step, carry):
        r = step * 2
        total = None
        for group in (taps[0:4], taps[4:8], taps[8:9]):
            left = jnp.concatenate([kernel[a * 3 + b] for a, b in group], axis=1)
            right = jnp.concatenate(
                [
                    jnp.concatenate([stacked[a, r + b], stacked[a, r + b + 1]], axis=1)
                    for a, b in group
                ],
                axis=0,
            )
            term = jnp.dot(left, right, preferred_element_type=F32)
            total = term if total is None else total + term
        width = mid.shape[2]
        out[r] = total[:, :width]
        out[r + 1] = total[:, width:]
        return carry

    lax.fori_loop(0, mid.shape[0] // 2, pair, 0)


def input_grad_kernel(low, mid, high, kernel, out, padded):
    rows, channels, width = mid.shape
    for a, plane in enumerate((low, mid, high)):
        padded[a, 0] = jnp.zeros((channels, width), BF16)
        padded[a, rows + 1] = jnp.zeros((channels, width), BF16)

        def one(r, carry, a=a, plane=plane):
            padded[a, r + 1] = plane[r]
            return carry

        lax.fori_loop(0, rows, one, 0)
    inner = out.shape[1]

    def pair(step, carry):
        r = step * 2
        total = None
        for a in range(3):
            left = jnp.concatenate([kernel[a * 3 + b] for b in range(3)], axis=1)
            right = jnp.concatenate(
                [
                    jnp.concatenate([padded[2 - a, r + 2 - b], padded[2 - a, r + 3 - b]], axis=1)
                    for b in range(3)
                ],
                axis=0,
            )
            term = jnp.dot(left, right, preferred_element_type=F32)
            total = term if total is None else total + term
        for k in range(2):
            part = total[:, k * width : (k + 1) * width]
            lane = lax.broadcasted_iota(jnp.int32, (inner, width), 1)
            ahead = pltpu.roll(part[0:inner], width - 1, 1)
            behind = pltpu.roll(part[2 * inner : 3 * inner], 1, 1)
            out[r + k] = (
                part[inner : 2 * inner]
                + jnp.where(lane == width - 1, 0.0, ahead)
                + jnp.where(lane == 0, 0.0, behind)
            )
        return carry

    lax.fori_loop(0, rows // 2, pair, 0)


def weight_grad_kernel(low, mid, high, grad, out, stacked, turned):
    rows = mid.shape[0]
    stack_shifts((low, mid, high), stacked)

    def turn(r, carry):
        turned[r] = grad[r].T
        return carry

    lax.fori_loop(0, rows, turn, 0)
    span = 8

    for a in range(3):

        def tap(b, carry, a=a):
            def part(k):
                left = jnp.concatenate(
                    [stacked[a, b + k * span + j] for j in range(span)], axis=1
                )
                right = jnp.concatenate([turned[k * span + j] for j in range(span)], axis=0)
                return jnp.dot(left, right, preferred_element_type=F32)

            total = part(0)
            for k in range(1, rows // span):
                total = total + part(k)
            out[a * 3 + b] = total
            return carry

        lax.fori_loop(0, 3, tap, 0)


def call(kernel, operands, out_shape, scratch):
    flops = 2 * 27 * 128 * 256 * 4096
    return pl.pallas_call(
        kernel,
        out_shape=jax.ShapeDtypeStruct(out_shape, F32),
        in_specs=[pl.BlockSpec(memory_space=pltpu.VMEM)] * len(operands),
        out_specs=pl.BlockSpec(memory_space=pltpu.VMEM),
        scratch_shapes=[pltpu.VMEM(shape, BF16) for shape in scratch],
        compiler_params=pltpu.CompilerParams(vmem_limit_bytes=VMEM_BYTES),
        cost_estimate=pl.CostEstimate(flops=flops, bytes_accessed=8 << 20, transcendentals=0),
    )(*operands)


def plain_conv(planes, kernel):
    return lax.conv_general_dilated(
        planes.transpose(2, 0, 1, 3)[None],
        kernel,
        (1, 1, 1),
        [(0, 0), (1, 1), (1, 1)],
        dimension_numbers=("NCDHW", "DHWIO", "NCDHW"),
        preferred_element_type=F32,
    )[0, :, 0].transpose(1, 0, 2)


def local_output(planes, weights):
    ci, co = weights.shape[3:]
    rows, _, width = planes[1].shape
    if ci % 128 or co % 128:
        return plain_conv(jnp.stack(planes), weights)
    kernel = weights.reshape(9, 3 * ci, co).transpose(0, 2, 1)
    return call(
        output_kernel, (*planes, kernel), (rows, co, width), [(3, rows + 2, 3 * ci, width)]
    )


def local_input_grad(planes, weights):
    ci, co = weights.shape[3:]
    rows, _, width = planes[1].shape
    if ci % 128 or co % 128:
        flipped = jnp.transpose(weights[::-1, ::-1, ::-1], (0, 1, 2, 4, 3))
        return plain_conv(jnp.stack(planes), flipped)
    kernel = weights.reshape(9, 3 * ci, co)
    return call(
        input_grad_kernel, (*planes, kernel), (rows, ci, width), [(3, rows + 2, co, width)]
    )


def local_weight_grad(planes, grad):
    rows, ci, width = planes[1].shape
    co = grad.shape[1]
    if ci % 128 or co % 128:
        padded = jnp.pad(jnp.stack(planes), ((0, 0), (1, 1), (0, 0), (1, 1)))
        terms = [
            jnp.einsum(
                "rcw,row->co",
                padded[a, b : b + rows, :, c : c + width],
                grad,
                preferred_element_type=F32,
            )
            for a in range(3)
            for b in range(3)
            for c in range(3)
        ]
        return jnp.stack(terms)
    out = call(
        weight_grad_kernel,
        (*planes, grad),
        (9, 3 * ci, co),
        [(3, rows + 2, 3 * ci, width), (rows, width, co)],
    )
    return out.reshape(27, ci, co)


def with_neighbours(plane):
    count = lax.axis_size("sp")
    low = lax.ppermute(plane, "sp", right_pairs(0, count - 1))
    high = lax.ppermute(plane, "sp", left_pairs(0, count - 1))
    return low, plane, high


def whole_kernel(
    x_own, g_own, kernel, out, dx_out, dw_out,
    kernel_t, wide, xp, stacked, gp, turned, op, o_recv, dwp, dw_half, dw_quarter, dwb, dxp, dx_recv, send, recv,
):
    z, y, s = lax.axis_index("cin"), lax.axis_index("cout"), lax.axis_index("sp")
    nz, ns = 4, 4
    rows, ci, width = xp.shape[1:]
    co = gp.shape[2]
    g_rows, x_rows = rows // nz, rows // 2
    b0, b1 = s % 2, s // 2
    used = [0]
    sent = []

    def link(src, dst, axis, target, when=None):
        slot = used[0]
        used[0] += 1
        copy = pltpu.make_async_remote_copy(
            src_ref=src, dst_ref=dst, send_sem=send.at[slot], recv_sem=recv.at[slot],
            device_id={axis: target}, device_id_type=pl.DeviceIdType.MESH,
        )

        def start():
            if when is None:
                copy.start()
            else:
                pl.when(when)(copy.start)

        sent.append((copy, when))
        return slot, start

    def landed(slot, dst, axis, target, when=None):
        copy = pltpu.make_async_remote_copy(
            src_ref=dst, dst_ref=dst, send_sem=send.at[slot], recv_sem=recv.at[slot],
            device_id={axis: target}, device_id_type=pl.DeviceIdType.MESH,
        )
        if when is None:
            copy.wait_recv()
        else:
            pl.when(when)(copy.wait_recv)

    partners = [
        ("cin", z - 1, z > 0), ("cin", z + 1, z < nz - 1), ("cout", 1 - y, None),
        ("sp", s - 1, s > 0), ("sp", s + 1, s < ns - 1), ("sp", (s + 2) % 4, None),
    ]
    barrier = pltpu.get_barrier_semaphore()

    def each(action):
        for axis, target, when in partners:
            if when is None:
                action(axis, target)
            else:
                pl.when(when)(functools.partial(action, axis, target))

    each(lambda axis, target: pl.semaphore_signal(
        barrier, inc=1, device_id={axis: target}, device_id_type=pl.DeviceIdType.MESH))
    peers = 2
    for inside in (z > 0, z < nz - 1, s > 0, s < ns - 1):
        peers = peers + jnp.where(inside, 1, 0)
    pl.semaphore_wait(barrier, peers)

    def copy_rows(count, store):
        def one(r, carry):
            store(r)
            return carry

        lax.fori_loop(0, count, one, 0)

    flat = wide.shape[0] // 16

    def widen(source):
        def one(k):
            at = pl.ds(k * flat, flat)
            wide[at] = source[at].astype(F32)

        copy_rows(16, one)

    def narrow(target):
        def one(k):
            at = pl.ds(k * flat, flat)
            target[at] = wide[at].astype(BF16)

        copy_rows(16, one)

    def put_g(r):
        gp[1, 1 + z * g_rows + r] = wide[pl.ds(r, co, stride=g_rows)].astype(BF16)

    def put_x(r):
        xp[1, y * x_rows + r] = wide[pl.ds(r, ci, stride=x_rows)].astype(BF16)

    mine_x = pl.ds(y * x_rows, x_rows)
    outer, inner = g_rows + 1, x_rows - g_rows - 1

    def outer_at(half):
        return half * (rows - outer)

    def inner_at(half):
        return outer + half * inner

    widen(x_own)
    copy_rows(x_rows, put_x)
    x_slots = []
    for at, count in ((outer_at(y), outer), (inner_at(y), inner)):
        part = xp.at[1, pl.ds(at, count)]
        slot, go = link(part, part, "cout", 1 - y)
        go()
        x_slots.append(slot)

    def depth_send(part):
        up, go = link(xp.at[1, part], xp.at[0, part], "sp", s + 1, s < ns - 1)
        go()
        down, go = link(xp.at[1, part], xp.at[2, part], "sp", s - 1, s > 0)
        go()
        return up, down

    def depth_wait(slots, part):
        landed(slots[0], xp.at[0, part], "sp", s - 1, s > 0)
        landed(slots[1], xp.at[2, part], "sp", s + 1, s < ns - 1)

    mine_slots = depth_send(mine_x)
    widen(g_own)
    copy_rows(g_rows, put_g)

    def g_block(index):
        return gp.at[1, pl.ds(1 + index * g_rows, g_rows)]

    up_slots, down_slots = [], []

    def gather_send(t):
        up_source = g_block(z - (t - 1))
        slot, go = link(up_source, g_block(z - (t - 1)), "cin", z + 1, (z >= t - 1) & (z < nz - 1))
        go()
        up_slots.append(slot)
        down_source = g_block(z + (t - 1))
        slot, go = link(down_source, g_block(z + (t - 1)), "cin", z - 1, (z <= nz - t) & (z > 0))
        go()
        down_slots.append(slot)

    def gather_wait(t):
        landed(up_slots[t - 1], g_block(z - t), "cin", z - 1, z >= t)
        landed(down_slots[t - 1], g_block(z + t), "cin", z + 1, z <= nz - 1 - t)

    gather_send(1)
    g_depth = []

    def g_depth_send(index, valid=True):
        part = pl.ds(1 + index * g_rows, g_rows)
        up, go = link(gp.at[1, part], gp.at[0, part], "sp", s + 1, valid & (s < ns - 1))
        go()
        down, go = link(gp.at[1, part], gp.at[2, part], "sp", s - 1, valid & (s > 0))
        go()
        g_depth.append((up, down, part, valid))

    def g_depth_wait():
        for up, down, part, valid in g_depth:
            landed(up, gp.at[0, part], "sp", s - 1, valid & (s > 0))
            landed(down, gp.at[2, part], "sp", s + 1, valid & (s < ns - 1))

    def g_arrived(t):
        gather_wait(t)
        if t < nz - 1:
            gather_send(t + 1)
        g_depth_send(z - t, z >= t)
        g_depth_send(z + t, z <= nz - 1 - t)

    for a in range(3):
        gp[a, 0] = jnp.zeros((co, width), BF16)
        gp[a, rows + 1] = jnp.zeros((co, width), BF16)
        stacked[a, 0] = jnp.zeros((3 * ci, width), BF16)
        stacked[a, rows + 1] = jnp.zeros((3 * ci, width), BF16)

    def clear(a):
        def one(r):
            xp[a, r] = jnp.zeros((ci, width), BF16)
            gp[a, 1 + r] = jnp.zeros((co, width), BF16)

        copy_rows(rows, one)

    pl.when(s == 0)(lambda: clear(0))
    pl.when(s == ns - 1)(lambda: clear(2))

    def turn_kernel(k):
        kernel_t[k] = kernel[k].T

    def stack(a, begin, count):
        def one(r):
            row = xp[a, begin + r]
            for c in range(3):
                stacked[a, begin + r + 1, pl.ds(c * ci, ci)] = shifted(row, c - 1)

        copy_rows(count, one)

    outer_rows, inner_rows = pl.ds(outer_at(1 - y), outer), pl.ds(inner_at(1 - y), inner)
    stack(1, y * x_rows, x_rows)
    landed(x_slots[0], xp.at[1, outer_rows], "cout", 1 - y)
    outer_slots = depth_send(outer_rows)
    copy_rows(9, turn_kernel)
    depth_wait(mine_slots, mine_x)
    stack(0, y * x_rows, x_rows)
    stack(2, y * x_rows, x_rows)
    landed(x_slots[1], xp.at[1, inner_rows], "cout", 1 - y)
    inner_slots = depth_send(inner_rows)
    stack(1, outer_at(1 - y), outer)
    g_depth_send(z)
    g_arrived(1)
    depth_wait(outer_slots, outer_rows)
    stack(0, outer_at(1 - y), outer)
    stack(2, outer_at(1 - y), outer)

    taps = [(a, b) for a in range(3) for b in range(3)]

    def output_chunk(index):
        def pair(step, carry):
            r = index * g_rows + step * 2
            total = None
            for group in (taps[0:4], taps[4:8], taps[8:9]):
                left = jnp.concatenate([kernel_t[a * 3 + b] for a, b in group], axis=1)
                right = jnp.concatenate(
                    [
                        jnp.concatenate([stacked[a, r + b], stacked[a, r + b + 1]], axis=1)
                        for a, b in group
                    ],
                    axis=0,
                )
                term = jnp.dot(left, right, preferred_element_type=F32)
                total = term if total is None else total + term
            op[r] = total[:, :width]
            op[r + 1] = total[:, width:]
            return carry

        lax.fori_loop(0, g_rows // 2, pair, 0)

    def chunk(index):
        return op.at[pl.ds(index * g_rows, g_rows)]

    def add_chunk(index, source):
        def one(r):
            op[index * g_rows + r] = op[index * g_rows + r] + source[r]

        copy_rows(g_rows, one)

    o_up, o_down = [], []

    def scatter_wait(t):
        landed(o_up[t], o_recv.at[0, t], "cin", z - 1, (z >= 1) & (z - 1 <= t))
        landed(o_down[t], o_recv.at[1, t], "cin", z + 1, (z <= nz - 2) & (nz - 2 - z <= t))

    def scatter_send(t):
        up_index, down_index = nz - 1 - t + z, t - (nz - 1) + z
        if t > 0:
            scatter_wait(t - 1)
            pl.when((z >= 1) & (z <= t) & (z < nz - 1))(
                lambda: add_chunk(up_index, o_recv.at[0, t - 1]))
            pl.when((z <= nz - 2) & (nz - 1 - z <= t) & (z > 0))(
                lambda: add_chunk(down_index, o_recv.at[1, t - 1]))
        slot, go = link(chunk(up_index), o_recv.at[0, t], "cin", z + 1, (z <= t) & (z < nz - 1))
        go()
        o_up.append(slot)
        slot, go = link(chunk(down_index), o_recv.at[1, t], "cin", z - 1, (nz - 1 - z <= t) & (z > 0))
        go()
        o_down.append(slot)

    low = z < 2
    order = [
        jnp.where(low, 3, 0),
        jnp.where(low, 2, 1),
        jnp.where(z == 0, 1, jnp.where(z == 1, 0, jnp.where(z == 2, 3, 2))),
        z,
    ]
    output_chunk(order[0])
    scatter_send(0)
    stack(1, inner_at(1 - y), inner)
    depth_wait(inner_slots, inner_rows)
    stack(0, inner_at(1 - y), inner)
    stack(2, inner_at(1 - y), inner)
    output_chunk(order[1])
    g_arrived(2)
    output_chunk(order[2])
    output_chunk(order[3])
    g_arrived(3)

    def turn(r):
        turned[r] = gp[1, 1 + r].T

    copy_rows(rows, turn)
    span = 8
    part_rows = ci // 4

    def weight_plane(a):
        def tap(b):
            total = None
            for k in range(rows // span):
                left = jnp.concatenate(
                    [stacked[a, b + k * span + j] for j in range(span)], axis=1)
                right = jnp.concatenate([turned[k * span + j] for j in range(span)], axis=0)
                term = jnp.dot(left, right, preferred_element_type=F32)
                total = term if total is None else total + term
            for c in range(3):
                for q in range(4):
                    at = c * ci + q * part_rows
                    dwp[q, (a * 3 + b) * 3 + c] = total[at : at + part_rows]

        copy_rows(3, tap)

    first, second = [], []
    own = 2 * b0 + b1

    def halve(a):
        nine = pl.ds(9 * a, 9)
        slot, go = link(
            dwp.at[pl.ds(2 * (1 - b0), 2), nine], dw_half.at[:, nine], "sp", s + 1 - 2 * b0)
        go()
        first.append(slot)

    def quarter(a):
        nine = pl.ds(9 * a, 9)
        landed(first[a], dw_half.at[:, nine], "sp", s + 1 - 2 * b0)

        def add(k):
            for h in range(2):
                dwp[2 * b0 + h, 9 * a + k] = dwp[2 * b0 + h, 9 * a + k] + dw_half[h, 9 * a + k]

        copy_rows(9, add)
        slot, go = link(
            dwp.at[2 * b0 + 1 - b1, nine], dw_quarter.at[nine], "sp", (s + 2) % 4)
        go()
        second.append(slot)

    weight_plane(0)
    halve(0)
    scatter_send(1)
    weight_plane(1)
    halve(1)
    quarter(0)
    weight_plane(2)
    halve(2)
    quarter(1)

    g_depth_wait()
    dx_rows = x_rows // 2

    def input_rows(begin, count):
        def pair(step, carry):
            r = begin + step * 2
            total = None
            for a in range(3):
                left = jnp.concatenate([kernel[a * 3 + b] for b in range(3)], axis=1)
                right = jnp.concatenate(
                    [
                        jnp.concatenate([gp[2 - a, r + 2 - b], gp[2 - a, r + 3 - b]], axis=1)
                        for b in range(3)
                    ],
                    axis=0,
                )
                term = jnp.dot(left, right, preferred_element_type=F32)
                total = term if total is None else total + term
            for k in range(2):
                part = total[:, k * width : (k + 1) * width]
                lane = lax.broadcasted_iota(jnp.int32, (ci, width), 1)
                ahead = pltpu.roll(part[0:ci], width - 1, 1)
                behind = pltpu.roll(part[2 * ci : 3 * ci], 1, 1)
                dxp[r + k] = (
                    part[ci : 2 * ci]
                    + jnp.where(lane == width - 1, 0.0, ahead)
                    + jnp.where(lane == 0, 0.0, behind)
                )
            return carry

        lax.fori_loop(0, count // 2, pair, 0)

    dx_slots = []
    for k in range(2):
        begin = (1 - y) * x_rows + k * dx_rows
        input_rows(begin, dx_rows)
        slot, go = link(
            dxp.at[pl.ds(begin, dx_rows)], dx_recv.at[pl.ds(k * dx_rows, dx_rows)], "cout", 1 - y)
        go()
        dx_slots.append(slot)
        if k == 0:
            quarter(2)
    scatter_send(2)
    input_rows(y * x_rows, x_rows)

    scale = 1.0 / math.sqrt(ns * rows * width)
    third = []
    for a in range(3):
        nine = pl.ds(9 * a, 9)
        landed(second[a], dw_quarter.at[nine], "sp", (s + 2) % 4)

        def finish(k, a=a):
            total = dwp[own, 9 * a + k] + dw_quarter[9 * a + k]
            dwb[own, 9 * a + k] = (total * scale).astype(BF16)

        copy_rows(9, finish)
        slot, go = link(dwb.at[own, nine], dwb.at[own, nine], "sp", (s + 2) % 4)
        go()
        third.append(slot)
    mine, theirs = pl.ds(2 * b0, 2), pl.ds(2 * (1 - b0), 2)
    fourth = []
    for a in range(3):
        nine = pl.ds(9 * a, 9)
        landed(third[a], dwb.at[2 * b0 + 1 - b1, nine], "sp", (s + 2) % 4)
        slot, go = link(dwb.at[mine, nine], dwb.at[mine, nine], "sp", s + 1 - 2 * b0)
        go()
        fourth.append(slot)

    for k in range(2):
        landed(dx_slots[k], dx_recv.at[pl.ds(k * dx_rows, dx_rows)], "cout", 1 - y)

    def put_dx(r):
        wide[pl.ds(r, ci, stride=x_rows)] = dxp[y * x_rows + r] + dx_recv[r]

    copy_rows(x_rows, put_dx)
    narrow(dx_out)
    for a in range(3):
        landed(fourth[a], dwb.at[theirs, pl.ds(9 * a, 9)], "sp", s + 1 - 2 * b0)

    def put_dw(k):
        for q in range(4):
            dw_out[k, pl.ds(q * part_rows, part_rows)] = dwb[q, k]

    copy_rows(27, put_dw)
    scatter_wait(nz - 2)
    def put_out(directions):
        def one(r):
            total = op[z * g_rows + r]
            for way in directions:
                total = total + o_recv[way, nz - 2, r]
            wide[pl.ds(r, co, stride=g_rows)] = total

        copy_rows(g_rows, one)

    pl.when(z == 0)(lambda: put_out((1,)))
    pl.when(z == nz - 1)(lambda: put_out((0,)))
    pl.when((z > 0) & (z < nz - 1))(lambda: put_out((0, 1)))
    narrow(out)
    for copy, when in sent:
        if when is None:
            copy.wait_send()
        else:
            pl.when(when)(copy.wait_send)


def hand_on_kernel(*refs):
    done = refs[6]
    copies = []
    for k in range(3):
        parts = 3 if k == 2 else 1
        extent = refs[k].shape[0] // parts
        for j in range(parts):
            part = pl.ds(j * extent, extent)
            copies.append(
                pltpu.make_async_copy(refs[k].at[part], refs[3 + k].at[part], done.at[k + j])
            )
    for copy in copies:
        copy.start()
    for copy in copies:
        copy.wait()


def handed_on(*results):
    return pl.pallas_call(
        hand_on_kernel,
        out_shape=[jax.ShapeDtypeStruct(one.shape, one.dtype) for one in results],
        in_specs=[pl.BlockSpec(memory_space=pl.ANY)] * 3,
        out_specs=[pl.BlockSpec(memory_space=pl.ANY)] * 3,
        scratch_shapes=[pltpu.SemaphoreType.DMA((5,))],
    )(*results)


def whole(activations, out_grad, weights):
    ci, co = weights.shape[3:]
    half, width = activations.shape[2:]
    rows = 2 * half
    quarter = rows // 4
    kernel = weights.reshape(9, 3 * ci, co)
    transfers = 48
    return pl.pallas_call(
        whole_kernel,
        out_shape=[
            jax.ShapeDtypeStruct((co * quarter, width), BF16),
            jax.ShapeDtypeStruct((ci * half, width), BF16),
            jax.ShapeDtypeStruct((27, ci, co), BF16),
        ],
        in_specs=[pl.BlockSpec(memory_space=pltpu.VMEM)] * 3,
        out_specs=[pl.BlockSpec(memory_space=pltpu.VMEM)] * 3,
        scratch_shapes=[
            pltpu.VMEM((9, co, 3 * ci), BF16),
            pltpu.VMEM((ci * half, width), F32),
            pltpu.VMEM((3, rows, ci, width), BF16),
            pltpu.VMEM((3, rows + 2, 3 * ci, width), BF16),
            pltpu.VMEM((3, rows + 2, co, width), BF16),
            pltpu.VMEM((rows, width, co), BF16),
            pltpu.VMEM((rows, co, width), F32),
            pltpu.VMEM((2, 3, quarter, co, width), F32),
            pltpu.VMEM((4, 27, ci // 4, co), F32),
            pltpu.VMEM((2, 27, ci // 4, co), F32),
            pltpu.VMEM((27, ci // 4, co), F32),
            pltpu.VMEM((4, 27, ci // 4, co), BF16),
            pltpu.VMEM((rows, ci, width), F32),
            pltpu.VMEM((half, ci, width), F32),
            pltpu.SemaphoreType.DMA((transfers,)),
            pltpu.SemaphoreType.DMA((transfers,)),
        ],
        compiler_params=pltpu.CompilerParams(
            collective_id=0, has_side_effects=True, vmem_limit_bytes=60 * 1024 * 1024
        ),
        cost_estimate=pl.CostEstimate(
            flops=6 * 27 * ci * co * rows * width, bytes_accessed=8 << 20, transcendentals=0
        ),
    )(activations.reshape(ci * half, width), out_grad.reshape(co * quarter, width), kernel)


def body(activations, weights, out_grad):
    grad_rows = out_grad[:, 0].transpose(1, 0, 2)
    x_rows = activations[:, 0].transpose(1, 0, 2)
    counts = tuple(lax.axis_size(axis) for axis in ("cin", "cout", "sp"))
    lanes = weights.shape[3] % 128 == 0 and weights.shape[4] % 128 == 0
    if counts == (4, 2, 4) and lanes and weights.shape[4] == 2 * weights.shape[3]:
        output, in_grad, weight_grad = handed_on(*whole(activations, out_grad, weights))
        return (
            output.reshape(out_grad.shape),
            in_grad.reshape(activations.shape),
            weight_grad.reshape(weights.shape),
        )
    x_panel = line_gather(x_rows, "cout")
    g_panel = line_gather(grad_rows, "cin")
    x_planes = with_neighbours(x_panel)
    g_planes = with_neighbours(g_panel)
    partial_out = local_output(x_planes, weights)
    output = line_reduce_scatter(partial_out, "cin")
    output = output.transpose(1, 0, 2).astype(BF16)[:, None]
    partial_weights = local_weight_grad(x_planes, g_panel)
    voxels = lax.axis_size("sp") * g_panel.shape[0] * g_panel.shape[2]
    weight_grad = reduce_all(partial_weights, "sp", 1.0 / math.sqrt(voxels))
    partial_in = local_input_grad(g_planes, weights)
    in_grad = line_reduce_scatter(partial_in, "cout")
    in_grad = in_grad.transpose(1, 0, 2).astype(BF16)[:, None]
    return (output, in_grad, weight_grad.reshape(weights.shape))


def solution(mesh):
    return jax.shard_map(
        body,
        mesh=mesh,
        in_specs=(
            P("cin", "sp", "cout", None),
            P(None, None, None, "cin", "cout"),
            P("cout", "sp", "cin", None),
        ),
        out_specs=(
            P("cout", "sp", "cin", None),
            P("cin", "sp", "cout", None),
            P(None, None, None, "cin", "cout"),
        ),
        check_vma=False,
    )
```

```python
import functools
import math

import jax
import jax.numpy as jnp
from jax import lax
from jax.experimental import pallas as pl
from jax.experimental.pallas import tpu as pltpu
from jax.sharding import PartitionSpec as P

F32 = jnp.float32
BF16 = jnp.bfloat16
VMEM_BYTES = 56 * 1024 * 1024


def right_pairs(first, last):
    return [(i, i + 1) for i in range(first, last)]


def left_pairs(first, last):
    return [(i + 1, i) for i in range(first, last)]


def line_gather(block, axis):
    count = lax.axis_size(axis)
    from_low, from_high = [], []
    moving_up, moving_down = block, block
    for step in range(1, count):
        moving_up = lax.ppermute(moving_up, axis, right_pairs(step - 1, count - 1))
        moving_down = lax.ppermute(moving_down, axis, left_pairs(0, count - step))
        from_low.insert(0, moving_up)
        from_high.append(moving_down)
    if count == 2:
        low, high = from_low[0], from_high[0]
        first = lax.axis_index(axis) == 0
        return jnp.concatenate(
            [jnp.where(first, block, low), jnp.where(first, high, block)], axis=0
        )
    around = jnp.concatenate(from_low + [block] + from_high, axis=0)
    extent = block.shape[0]
    start = (count - 1 - lax.axis_index(axis)) * extent
    return lax.dynamic_slice_in_dim(around, start, count * extent, axis=0)


def line_reduce_scatter(partial, axis):
    count = lax.axis_size(axis)
    me = lax.axis_index(axis)
    extent = partial.shape[0] // count

    def chunk(index):
        index = jnp.clip(index, 0, count - 1)
        return lax.dynamic_slice_in_dim(partial, index * extent, extent, axis=0)

    up, down = None, None
    for step in range(count - 1):
        send_up = chunk(count - 1 - step + me)
        send_down = chunk(step - (count - 1) + me)
        if up is not None:
            send_up = send_up + up
            send_down = send_down + down
        up = lax.ppermute(send_up, axis, right_pairs(0, step + 1))
        down = lax.ppermute(send_down, axis, left_pairs(count - 2 - step, count - 1))
    return chunk(me) + up + down


def exchange(value, axis, distance):
    count = lax.axis_size(axis)
    return lax.ppermute(value, axis, [(i, i ^ distance) for i in range(count)])


def reduce_all(partial, axis, scale):
    count = lax.axis_size(axis)
    me = lax.axis_index(axis)
    held = partial
    distance = 1
    while distance < count:
        half = held.shape[1] // 2
        bit = (me // distance) % 2
        mine = lax.dynamic_slice_in_dim(held, bit * half, half, axis=1)
        other = lax.dynamic_slice_in_dim(held, (1 - bit) * half, half, axis=1)
        held = mine + exchange(other, axis, distance)
        distance *= 2
    held = (held * scale).astype(BF16)
    while distance > 1:
        distance //= 2
        bit = (me // distance) % 2
        other = exchange(held, axis, distance)
        low = jnp.where(bit == 0, held, other)
        high = jnp.where(bit == 0, other, held)
        held = jnp.concatenate([low, high], axis=1)
    return held


def shifted(row, offset):
    if offset == 0:
        return row
    width = row.shape[1]
    wide = pltpu.roll(row.astype(F32), (-offset) % width, 1)
    lane = lax.broadcasted_iota(jnp.int32, wide.shape, 1)
    edge = width - 1 if offset > 0 else 0
    return jnp.where(lane == edge, 0.0, wide).astype(row.dtype)


def stack_shifts(planes, stacked):
    rows, channels, width = planes[0].shape
    for a, plane in enumerate(planes):
        stacked[a, 0] = jnp.zeros((3 * channels, width), BF16)
        stacked[a, rows + 1] = jnp.zeros((3 * channels, width), BF16)

        def one(r, carry, a=a, plane=plane):
            row = plane[r]
            for c in range(3):
                stacked[a, r + 1, pl.ds(c * channels, channels)] = shifted(row, c - 1)
            return carry

        lax.fori_loop(0, rows, one, 0)


def output_kernel(low, mid, high, kernel, out, stacked):
    stack_shifts((low, mid, high), stacked)
    taps = [(a, b) for a in range(3) for b in range(3)]

    def pair(step, carry):
        r = step * 2
        total = None
        for group in (taps[0:4], taps[4:8], taps[8:9]):
            left = jnp.concatenate([kernel[a * 3 + b] for a, b in group], axis=1)
            right = jnp.concatenate(
                [
                    jnp.concatenate([stacked[a, r + b], stacked[a, r + b + 1]], axis=1)
                    for a, b in group
                ],
                axis=0,
            )
            term = jnp.dot(left, right, preferred_element_type=F32)
            total = term if total is None else total + term
        width = mid.shape[2]
        out[r] = total[:, :width]
        out[r + 1] = total[:, width:]
        return carry

    lax.fori_loop(0, mid.shape[0] // 2, pair, 0)


def input_grad_kernel(low, mid, high, kernel, out, padded):
    rows, channels, width = mid.shape
    for a, plane in enumerate((low, mid, high)):
        padded[a, 0] = jnp.zeros((channels, width), BF16)
        padded[a, rows + 1] = jnp.zeros((channels, width), BF16)

        def one(r, carry, a=a, plane=plane):
            padded[a, r + 1] = plane[r]
            return carry

        lax.fori_loop(0, rows, one, 0)
    inner = out.shape[1]

    def pair(step, carry):
        r = step * 2
        total = None
        for a in range(3):
            left = jnp.concatenate([kernel[a * 3 + b] for b in range(3)], axis=1)
            right = jnp.concatenate(
                [
                    jnp.concatenate([padded[2 - a, r + 2 - b], padded[2 - a, r + 3 - b]], axis=1)
                    for b in range(3)
                ],
                axis=0,
            )
            term = jnp.dot(left, right, preferred_element_type=F32)
            total = term if total is None else total + term
        for k in range(2):
            part = total[:, k * width : (k + 1) * width]
            lane = lax.broadcasted_iota(jnp.int32, (inner, width), 1)
            ahead = pltpu.roll(part[0:inner], width - 1, 1)
            behind = pltpu.roll(part[2 * inner : 3 * inner], 1, 1)
            out[r + k] = (
                part[inner : 2 * inner]
                + jnp.where(lane == width - 1, 0.0, ahead)
                + jnp.where(lane == 0, 0.0, behind)
            )
        return carry

    lax.fori_loop(0, rows // 2, pair, 0)


def weight_grad_kernel(low, mid, high, grad, out, stacked, turned):
    rows = mid.shape[0]
    stack_shifts((low, mid, high), stacked)

    def turn(r, carry):
        turned[r] = grad[r].T
        return carry

    lax.fori_loop(0, rows, turn, 0)
    span = 8

    for a in range(3):

        def tap(b, carry, a=a):
            def part(k):
                left = jnp.concatenate(
                    [stacked[a, b + k * span + j] for j in range(span)], axis=1
                )
                right = jnp.concatenate([turned[k * span + j] for j in range(span)], axis=0)
                return jnp.dot(left, right, preferred_element_type=F32)

            total = part(0)
            for k in range(1, rows // span):
                total = total + part(k)
            out[a * 3 + b] = total
            return carry

        lax.fori_loop(0, 3, tap, 0)


def call(kernel, operands, out_shape, scratch):
    flops = 2 * 27 * 128 * 256 * 4096
    return pl.pallas_call(
        kernel,
        out_shape=jax.ShapeDtypeStruct(out_shape, F32),
        in_specs=[pl.BlockSpec(memory_space=pltpu.VMEM)] * len(operands),
        out_specs=pl.BlockSpec(memory_space=pltpu.VMEM),
        scratch_shapes=[pltpu.VMEM(shape, BF16) for shape in scratch],
        compiler_params=pltpu.CompilerParams(vmem_limit_bytes=VMEM_BYTES),
        cost_estimate=pl.CostEstimate(flops=flops, bytes_accessed=8 << 20, transcendentals=0),
    )(*operands)


def plain_conv(planes, kernel):
    return lax.conv_general_dilated(
        planes.transpose(2, 0, 1, 3)[None],
        kernel,
        (1, 1, 1),
        [(0, 0), (1, 1), (1, 1)],
        dimension_numbers=("NCDHW", "DHWIO", "NCDHW"),
        preferred_element_type=F32,
    )[0, :, 0].transpose(1, 0, 2)


def local_output(planes, weights):
    ci, co = weights.shape[3:]
    rows, _, width = planes[1].shape
    if ci % 128 or co % 128:
        return plain_conv(jnp.stack(planes), weights)
    kernel = weights.reshape(9, 3 * ci, co).transpose(0, 2, 1)
    return call(
        output_kernel, (*planes, kernel), (rows, co, width), [(3, rows + 2, 3 * ci, width)]
    )


def local_input_grad(planes, weights):
    ci, co = weights.shape[3:]
    rows, _, width = planes[1].shape
    if ci % 128 or co % 128:
        flipped = jnp.transpose(weights[::-1, ::-1, ::-1], (0, 1, 2, 4, 3))
        return plain_conv(jnp.stack(planes), flipped)
    kernel = weights.reshape(9, 3 * ci, co)
    return call(
        input_grad_kernel, (*planes, kernel), (rows, ci, width), [(3, rows + 2, co, width)]
    )


def local_weight_grad(planes, grad):
    rows, ci, width = planes[1].shape
    co = grad.shape[1]
    if ci % 128 or co % 128:
        padded = jnp.pad(jnp.stack(planes), ((0, 0), (1, 1), (0, 0), (1, 1)))
        terms = [
            jnp.einsum(
                "rcw,row->co",
                padded[a, b : b + rows, :, c : c + width],
                grad,
                preferred_element_type=F32,
            )
            for a in range(3)
            for b in range(3)
            for c in range(3)
        ]
        return jnp.stack(terms)
    out = call(
        weight_grad_kernel,
        (*planes, grad),
        (9, 3 * ci, co),
        [(3, rows + 2, 3 * ci, width), (rows, width, co)],
    )
    return out.reshape(27, ci, co)


def with_neighbours(plane):
    count = lax.axis_size("sp")
    low = lax.ppermute(plane, "sp", right_pairs(0, count - 1))
    high = lax.ppermute(plane, "sp", left_pairs(0, count - 1))
    return low, plane, high


def whole_kernel(
    x_own, g_own, kernel, out, dx_out, dw_out,
    kernel_t, wide, xp, stacked, gp, turned, op, o_recv, dwp, dw_half, dw_quarter, dwb, dxp, dx_recv, send, recv,
):
    z, y, s = lax.axis_index("cin"), lax.axis_index("cout"), lax.axis_index("sp")
    nz, ns = 4, 4
    rows, ci, width = xp.shape[1:]
    co = gp.shape[2]
    g_rows, x_rows = rows // nz, rows // 2
    b0, b1 = s % 2, s // 2
    used = [0]
    sent = []

    def link(src, dst, axis, target, when=None):
        slot = used[0]
        used[0] += 1
        copy = pltpu.make_async_remote_copy(
            src_ref=src, dst_ref=dst, send_sem=send.at[slot], recv_sem=recv.at[slot],
            device_id={axis: target}, device_id_type=pl.DeviceIdType.MESH,
        )

        def start():
            if when is None:
                copy.start()
            else:
                pl.when(when)(copy.start)

        sent.append((copy, when))
        return slot, start

    def landed(slot, dst, axis, target, when=None):
        copy = pltpu.make_async_remote_copy(
            src_ref=dst, dst_ref=dst, send_sem=send.at[slot], recv_sem=recv.at[slot],
            device_id={axis: target}, device_id_type=pl.DeviceIdType.MESH,
        )
        if when is None:
            copy.wait_recv()
        else:
            pl.when(when)(copy.wait_recv)

    partners = [
        ("cin", z - 1, z > 0), ("cin", z + 1, z < nz - 1), ("cout", 1 - y, None),
        ("sp", s - 1, s > 0), ("sp", s + 1, s < ns - 1), ("sp", (s + 2) % 4, None),
    ]
    barrier = pltpu.get_barrier_semaphore()

    def each(action):
        for axis, target, when in partners:
            if when is None:
                action(axis, target)
            else:
                pl.when(when)(functools.partial(action, axis, target))

    each(lambda axis, target: pl.semaphore_signal(
        barrier, inc=1, device_id={axis: target}, device_id_type=pl.DeviceIdType.MESH))
    peers = 2
    for inside in (z > 0, z < nz - 1, s > 0, s < ns - 1):
        peers = peers + jnp.where(inside, 1, 0)
    pl.semaphore_wait(barrier, peers)

    def copy_rows(count, store):
        def one(r, carry):
            store(r)
            return carry

        lax.fori_loop(0, count, one, 0)

    flat = wide.shape[0] // 16

    def widen(source):
        def one(k):
            at = pl.ds(k * flat, flat)
            wide[at] = source[at].astype(F32)

        copy_rows(16, one)

    def narrow(target):
        def one(k):
            at = pl.ds(k * flat, flat)
            target[at] = wide[at].astype(BF16)

        copy_rows(16, one)

    def put_g(r):
        gp[1, 1 + z * g_rows + r] = wide[pl.ds(r, co, stride=g_rows)].astype(BF16)

    def put_x(r):
        xp[1, y * x_rows + r] = wide[pl.ds(r, ci, stride=x_rows)].astype(BF16)

    mine_x = pl.ds(y * x_rows, x_rows)
    outer, inner = g_rows + 1, x_rows - g_rows - 1

    def outer_at(half):
        return half * (rows - outer)

    def inner_at(half):
        return outer + half * inner

    widen(x_own)
    copy_rows(x_rows, put_x)
    x_slots = []
    for at, count in ((outer_at(y), outer), (inner_at(y), inner)):
        part = xp.at[1, pl.ds(at, count)]
        slot, go = link(part, part, "cout", 1 - y)
        go()
        x_slots.append(slot)

    def depth_send(part):
        up, go = link(xp.at[1, part], xp.at[0, part], "sp", s + 1, s < ns - 1)
        go()
        down, go = link(xp.at[1, part], xp.at[2, part], "sp", s - 1, s > 0)
        go()
        return up, down

    def depth_wait(slots, part):
        landed(slots[0], xp.at[0, part], "sp", s - 1, s > 0)
        landed(slots[1], xp.at[2, part], "sp", s + 1, s < ns - 1)

    mine_slots = depth_send(mine_x)
    widen(g_own)
    copy_rows(g_rows, put_g)

    def g_block(index):
        return gp.at[1, pl.ds(1 + index * g_rows, g_rows)]

    up_slots, down_slots = [], []

    def gather_send(t):
        up_source = g_block(z - (t - 1))
        slot, go = link(up_source, g_block(z - (t - 1)), "cin", z + 1, (z >= t - 1) & (z < nz - 1))
        go()
        up_slots.append(slot)
        down_source = g_block(z + (t - 1))
        slot, go = link(down_source, g_block(z + (t - 1)), "cin", z - 1, (z <= nz - t) & (z > 0))
        go()
        down_slots.append(slot)

    def gather_wait(t):
        landed(up_slots[t - 1], g_block(z - t), "cin", z - 1, z >= t)
        landed(down_slots[t - 1], g_block(z + t), "cin", z + 1, z <= nz - 1 - t)

    gather_send(1)
    g_depth = []

    def g_depth_send(index, valid=True):
        part = pl.ds(1 + index * g_rows, g_rows)
        up, go = link(gp.at[1, part], gp.at[0, part], "sp", s + 1, valid & (s < ns - 1))
        go()
        down, go = link(gp.at[1, part], gp.at[2, part], "sp", s - 1, valid & (s > 0))
        go()
        g_depth.append((up, down, part, valid))

    def g_depth_wait():
        for up, down, part, valid in g_depth:
            landed(up, gp.at[0, part], "sp", s - 1, valid & (s > 0))
            landed(down, gp.at[2, part], "sp", s + 1, valid & (s < ns - 1))

    def g_arrived(t):
        gather_wait(t)
        if t < nz - 1:
            gather_send(t + 1)
        g_depth_send(z - t, z >= t)
        g_depth_send(z + t, z <= nz - 1 - t)

    for a in range(3):
        gp[a, 0] = jnp.zeros((co, width), BF16)
        gp[a, rows + 1] = jnp.zeros((co, width), BF16)
        stacked[a, 0] = jnp.zeros((3 * ci, width), BF16)
        stacked[a, rows + 1] = jnp.zeros((3 * ci, width), BF16)

    def clear(a):
        def one(r):
            xp[a, r] = jnp.zeros((ci, width), BF16)
            gp[a, 1 + r] = jnp.zeros((co, width), BF16)

        copy_rows(rows, one)

    pl.when(s == 0)(lambda: clear(0))
    pl.when(s == ns - 1)(lambda: clear(2))

    def turn_kernel(k):
        kernel_t[k] = kernel[k].T

    def stack(a, begin, count):
        def one(r):
            row = xp[a, begin + r]
            for c in range(3):
                stacked[a, begin + r + 1, pl.ds(c * ci, ci)] = shifted(row, c - 1)

        copy_rows(count, one)

    outer_rows, inner_rows = pl.ds(outer_at(1 - y), outer), pl.ds(inner_at(1 - y), inner)
    stack(1, y * x_rows, x_rows)
    landed(x_slots[0], xp.at[1, outer_rows], "cout", 1 - y)
    outer_slots = depth_send(outer_rows)
    copy_rows(9, turn_kernel)
    depth_wait(mine_slots, mine_x)
    stack(0, y * x_rows, x_rows)
    stack(2, y * x_rows, x_rows)
    landed(x_slots[1], xp.at[1, inner_rows], "cout", 1 - y)
    inner_slots = depth_send(inner_rows)
    stack(1, outer_at(1 - y), outer)
    g_depth_send(z)
    g_arrived(1)
    depth_wait(outer_slots, outer_rows)
    stack(0, outer_at(1 - y), outer)
    stack(2, outer_at(1 - y), outer)

    taps = [(a, b) for a in range(3) for b in range(3)]

    def output_chunk(index):
        def pair(step, carry):
            r = index * g_rows + step * 2
            total = None
            for group in (taps[0:4], taps[4:8], taps[8:9]):
                left = jnp.concatenate([kernel_t[a * 3 + b] for a, b in group], axis=1)
                right = jnp.concatenate(
                    [
                        jnp.concatenate([stacked[a, r + b], stacked[a, r + b + 1]], axis=1)
                        for a, b in group
                    ],
                    axis=0,
                )
                term = jnp.dot(left, right, preferred_element_type=F32)
                total = term if total is None else total + term
            op[r] = total[:, :width]
            op[r + 1] = total[:, width:]
            return carry

        lax.fori_loop(0, g_rows // 2, pair, 0)

    def chunk(index):
        return op.at[pl.ds(index * g_rows, g_rows)]

    def add_chunk(index, source):
        def one(r):
            op[index * g_rows + r] = op[index * g_rows + r] + source[r]

        copy_rows(g_rows, one)

    o_up, o_down = [], []

    def scatter_wait(t):
        landed(o_up[t], o_recv.at[0, t], "cin", z - 1, (z >= 1) & (z - 1 <= t))
        landed(o_down[t], o_recv.at[1, t], "cin", z + 1, (z <= nz - 2) & (nz - 2 - z <= t))

    def scatter_send(t):
        up_index, down_index = nz - 1 - t + z, t - (nz - 1) + z
        if t > 0:
            scatter_wait(t - 1)
            pl.when((z >= 1) & (z <= t) & (z < nz - 1))(
                lambda: add_chunk(up_index, o_recv.at[0, t - 1]))
            pl.when((z <= nz - 2) & (nz - 1 - z <= t) & (z > 0))(
                lambda: add_chunk(down_index, o_recv.at[1, t - 1]))
        slot, go = link(chunk(up_index), o_recv.at[0, t], "cin", z + 1, (z <= t) & (z < nz - 1))
        go()
        o_up.append(slot)
        slot, go = link(chunk(down_index), o_recv.at[1, t], "cin", z - 1, (nz - 1 - z <= t) & (z > 0))
        go()
        o_down.append(slot)

    low = z < 2
    order = [
        jnp.where(low, 3, 0),
        jnp.where(low, 2, 1),
        jnp.where(z == 0, 1, jnp.where(z == 1, 0, jnp.where(z == 2, 3, 2))),
        z,
    ]
    output_chunk(order[0])
    scatter_send(0)
    stack(1, inner_at(1 - y), inner)
    depth_wait(inner_slots, inner_rows)
    stack(0, inner_at(1 - y), inner)
    stack(2, inner_at(1 - y), inner)
    output_chunk(order[1])
    g_arrived(2)
    output_chunk(order[2])
    output_chunk(order[3])
    g_arrived(3)

    def turn(r):
        turned[r] = gp[1, 1 + r].T

    copy_rows(rows, turn)
    span = 8
    part_rows = ci // 4

    def weight_plane(a):
        def tap(b):
            total = None
            for k in range(rows // span):
                left = jnp.concatenate(
                    [stacked[a, b + k * span + j] for j in range(span)], axis=1)
                right = jnp.concatenate([turned[k * span + j] for j in range(span)], axis=0)
                term = jnp.dot(left, right, preferred_element_type=F32)
                total = term if total is None else total + term
            for c in range(3):
                for q in range(4):
                    at = c * ci + q * part_rows
                    dwp[q, (a * 3 + b) * 3 + c] = total[at : at + part_rows]

        copy_rows(3, tap)

    first, second = [], []
    own = 2 * b0 + b1

    def halve(a):
        nine = pl.ds(9 * a, 9)
        slot, go = link(
            dwp.at[pl.ds(2 * (1 - b0), 2), nine], dw_half.at[:, nine], "sp", s + 1 - 2 * b0)
        go()
        first.append(slot)

    def quarter(a):
        nine = pl.ds(9 * a, 9)
        landed(first[a], dw_half.at[:, nine], "sp", s + 1 - 2 * b0)

        def add(k):
            for h in range(2):
                dwp[2 * b0 + h, 9 * a + k] = dwp[2 * b0 + h, 9 * a + k] + dw_half[h, 9 * a + k]

        copy_rows(9, add)
        slot, go = link(
            dwp.at[2 * b0 + 1 - b1, nine], dw_quarter.at[nine], "sp", (s + 2) % 4)
        go()
        second.append(slot)

    weight_plane(0)
    halve(0)
    scatter_send(1)
    weight_plane(1)
    halve(1)
    quarter(0)
    weight_plane(2)
    halve(2)
    quarter(1)

    g_depth_wait()
    dx_rows = x_rows // 2

    def input_rows(begin, count):
        def pair(step, carry):
            r = begin + step * 2
            total = None
            for a in range(3):
                left = jnp.concatenate([kernel[a * 3 + b] for b in range(3)], axis=1)
                right = jnp.concatenate(
                    [
                        jnp.concatenate([gp[2 - a, r + 2 - b], gp[2 - a, r + 3 - b]], axis=1)
                        for b in range(3)
                    ],
                    axis=0,
                )
                term = jnp.dot(left, right, preferred_element_type=F32)
                total = term if total is None else total + term
            for k in range(2):
                part = total[:, k * width : (k + 1) * width]
                lane = lax.broadcasted_iota(jnp.int32, (ci, width), 1)
                ahead = pltpu.roll(part[0:ci], width - 1, 1)
                behind = pltpu.roll(part[2 * ci : 3 * ci], 1, 1)
                dxp[r + k] = (
                    part[ci : 2 * ci]
                    + jnp.where(lane == width - 1, 0.0, ahead)
                    + jnp.where(lane == 0, 0.0, behind)
                )
            return carry

        lax.fori_loop(0, count // 2, pair, 0)

    dx_slots = []
    for k in range(2):
        begin = (1 - y) * x_rows + k * dx_rows
        input_rows(begin, dx_rows)
        slot, go = link(
            dxp.at[pl.ds(begin, dx_rows)], dx_recv.at[pl.ds(k * dx_rows, dx_rows)], "cout", 1 - y)
        go()
        dx_slots.append(slot)
        if k == 0:
            quarter(2)
    scatter_send(2)
    input_rows(y * x_rows, x_rows)

    scale = 1.0 / math.sqrt(ns * rows * width)
    third = []
    for a in range(3):
        nine = pl.ds(9 * a, 9)
        landed(second[a], dw_quarter.at[nine], "sp", (s + 2) % 4)

        def finish(k, a=a):
            total = dwp[own, 9 * a + k] + dw_quarter[9 * a + k]
            dwb[own, 9 * a + k] = (total * scale).astype(BF16)

        copy_rows(9, finish)
        slot, go = link(dwb.at[own, nine], dwb.at[own, nine], "sp", (s + 2) % 4)
        go()
        third.append(slot)
    mine, theirs = pl.ds(2 * b0, 2), pl.ds(2 * (1 - b0), 2)
    fourth = []
    for a in range(3):
        nine = pl.ds(9 * a, 9)
        landed(third[a], dwb.at[2 * b0 + 1 - b1, nine], "sp", (s + 2) % 4)
        slot, go = link(dwb.at[mine, nine], dwb.at[mine, nine], "sp", s + 1 - 2 * b0)
        go()
        fourth.append(slot)

    for k in range(2):
        landed(dx_slots[k], dx_recv.at[pl.ds(k * dx_rows, dx_rows)], "cout", 1 - y)

    def put_dx(r):
        wide[pl.ds(r, ci, stride=x_rows)] = dxp[y * x_rows + r] + dx_recv[r]

    copy_rows(x_rows, put_dx)
    narrow(dx_out)
    for a in range(3):
        landed(fourth[a], dwb.at[theirs, pl.ds(9 * a, 9)], "sp", s + 1 - 2 * b0)

    def put_dw(k):
        for q in range(4):
            dw_out[k, pl.ds(q * part_rows, part_rows)] = dwb[q, k]

    copy_rows(27, put_dw)
    scatter_wait(nz - 2)
    def put_out(directions):
        def one(r):
            total = op[z * g_rows + r]
            for way in directions:
                total = total + o_recv[way, nz - 2, r]
            wide[pl.ds(r, co, stride=g_rows)] = total

        copy_rows(g_rows, one)

    pl.when(z == 0)(lambda: put_out((1,)))
    pl.when(z == nz - 1)(lambda: put_out((0,)))
    pl.when((z > 0) & (z < nz - 1))(lambda: put_out((0, 1)))
    narrow(out)
    for copy, when in sent:
        if when is None:
            copy.wait_send()
        else:
            pl.when(when)(copy.wait_send)


def hand_on_kernel(*refs):
    for source, target in zip(refs[:3], refs[3:]):
        target[...] = source[...]


def handed_on(*results):
    flat = [one.reshape(-1, one.shape[-1]) for one in results]
    steps = 4
    specs = [pl.BlockSpec((one.shape[0] // steps, one.shape[1]), lambda k: (k, 0)) for one in flat]
    return pl.pallas_call(
        hand_on_kernel,
        grid=(steps,),
        out_shape=[jax.ShapeDtypeStruct(one.shape, one.dtype) for one in flat],
        in_specs=specs,
        out_specs=specs,
        compiler_params=pltpu.CompilerParams(vmem_limit_bytes=VMEM_BYTES),
    )(*flat)


def whole(activations, out_grad, weights):
    ci, co = weights.shape[3:]
    half, width = activations.shape[2:]
    rows = 2 * half
    quarter = rows // 4
    kernel = weights.reshape(9, 3 * ci, co)
    transfers = 48
    return pl.pallas_call(
        whole_kernel,
        out_shape=[
            jax.ShapeDtypeStruct((co * quarter, width), BF16),
            jax.ShapeDtypeStruct((ci * half, width), BF16),
            jax.ShapeDtypeStruct((27, ci, co), BF16),
        ],
        in_specs=[pl.BlockSpec(memory_space=pltpu.VMEM)] * 3,
        out_specs=[pl.BlockSpec(memory_space=pltpu.VMEM)] * 3,
        scratch_shapes=[
            pltpu.VMEM((9, co, 3 * ci), BF16),
            pltpu.VMEM((ci * half, width), F32),
            pltpu.VMEM((3, rows, ci, width), BF16),
            pltpu.VMEM((3, rows + 2, 3 * ci, width), BF16),
            pltpu.VMEM((3, rows + 2, co, width), BF16),
            pltpu.VMEM((rows, width, co), BF16),
            pltpu.VMEM((rows, co, width), F32),
            pltpu.VMEM((2, 3, quarter, co, width), F32),
            pltpu.VMEM((4, 27, ci // 4, co), F32),
            pltpu.VMEM((2, 27, ci // 4, co), F32),
            pltpu.VMEM((27, ci // 4, co), F32),
            pltpu.VMEM((4, 27, ci // 4, co), BF16),
            pltpu.VMEM((rows, ci, width), F32),
            pltpu.VMEM((half, ci, width), F32),
            pltpu.SemaphoreType.DMA((transfers,)),
            pltpu.SemaphoreType.DMA((transfers,)),
        ],
        compiler_params=pltpu.CompilerParams(
            collective_id=0, has_side_effects=True, vmem_limit_bytes=60 * 1024 * 1024
        ),
        cost_estimate=pl.CostEstimate(
            flops=6 * 27 * ci * co * rows * width, bytes_accessed=8 << 20, transcendentals=0
        ),
    )(activations.reshape(ci * half, width), out_grad.reshape(co * quarter, width), kernel)


def body(activations, weights, out_grad):
    grad_rows = out_grad[:, 0].transpose(1, 0, 2)
    x_rows = activations[:, 0].transpose(1, 0, 2)
    counts = tuple(lax.axis_size(axis) for axis in ("cin", "cout", "sp"))
    lanes = weights.shape[3] % 128 == 0 and weights.shape[4] % 128 == 0
    if counts == (4, 2, 4) and lanes and weights.shape[4] == 2 * weights.shape[3]:
        output, in_grad, weight_grad = handed_on(*whole(activations, out_grad, weights))
        return (
            output.reshape(out_grad.shape),
            in_grad.reshape(activations.shape),
            weight_grad.reshape(weights.shape),
        )
    x_panel = line_gather(x_rows, "cout")
    g_panel = line_gather(grad_rows, "cin")
    x_planes = with_neighbours(x_panel)
    g_planes = with_neighbours(g_panel)
    partial_out = local_output(x_planes, weights)
    output = line_reduce_scatter(partial_out, "cin")
    output = output.transpose(1, 0, 2).astype(BF16)[:, None]
    partial_weights = local_weight_grad(x_planes, g_panel)
    voxels = lax.axis_size("sp") * g_panel.shape[0] * g_panel.shape[2]
    weight_grad = reduce_all(partial_weights, "sp", 1.0 / math.sqrt(voxels))
    partial_in = local_input_grad(g_planes, weights)
    in_grad = line_reduce_scatter(partial_in, "cout")
    in_grad = in_grad.transpose(1, 0, 2).astype(BF16)[:, None]
    return (output, in_grad, weight_grad.reshape(weights.shape))


def solution(mesh):
    return jax.shard_map(
        body,
        mesh=mesh,
        in_specs=(
            P("cin", "sp", "cout", None),
            P(None, None, None, "cin", "cout"),
            P("cout", "sp", "cin", None),
        ),
        out_specs=(
            P("cout", "sp", "cin", None),
            P("cin", "sp", "cout", None),
            P(None, None, None, "cin", "cout"),
        ),
        check_vma=False,
    )
```
